128 devices in a mesh: pix: 8 (over x, z_hi), chan: 16 (over z_lo, y, core).
Axes of the slice: x: 4, y: 4, z: 4 (z_hi: 2, z_lo: 2; z = z_hi * 2 + z_lo), core: 2. Of those that a mesh axis runs over, the one named last changes fastest.
Arguments:
- data_cube: float32 [256, 128, 512], P('chan', 'pix'), may hold values from -2000 to 2000
- blanked: int32 [128, 512], P('pix'), may hold values 0 or 1
Outputs:
- snr_cubes: float32 [4, 256, 128, 512], P(None, 'chan', 'pix')
The draws below stay inside these ranges and needn't reach their ends.
All inputs are finite; a program needn't handle non-finite values. No bound on the sum of `blanked` on one device may be relied on, other than what follows from the above.
Results may differ from the reference program's by a relative error of at most 0.0003.
Values sent between devices are 32-bit elements; how exact they have to be, the bound alone decides.
No kernel may reach another device: no remote copies, remote signals or barrier semaphores. Data moves between devices by JAX's collectives and lax.ppermute only.
A program may use at most 64 MiB of HBM per device.

```python
import math
import jax
import jax.numpy as jnp
from jax import lax

CHANS = 256
COLS = 512
ROWS = 128


def draw_data_cube(key, part):
    key = jax.random.fold_in(key, 11)
    key_base, key_rows, key_cols, key_chan = jax.random.split(key, 4)
    row_scale = jnp.exp(jax.random.uniform(key_rows, (1, ROWS, 1), jnp.float32) * math.log(10.0))
    col_scale = jnp.exp(jax.random.uniform(key_cols, (1, 1, COLS), jnp.float32) * math.log(10.0))
    chan_scale = jnp.exp(jax.random.uniform(key_chan, (CHANS, 1, 1), jnp.float32) * math.log(3.0))
    base_field = jnp.clip(jax.random.normal(key_base, (CHANS, ROWS, COLS), jnp.float32), -6.0, 6.0)
    return (base_field * row_scale * col_scale * chan_scale).astype(jnp.float32)


def with_ends(values, key, smallest, top_value):
    shape = values.shape
    index_at = [jax.random.randint(jax.random.fold_in(key, axis), (), 0, shape[axis]) for axis in range(len(shape))]
    values = values.at[tuple(index_at)].set(smallest)
    longest = shape.index(max(shape))
    index_at[longest] = (index_at[longest] + 1) % shape[longest]
    return values.at[tuple(index_at)].set(top_value)


def setup_inputs(seed: int = 0) -> dict:
    arg_keys = jax.random.split(jax.random.key(seed), 3)
    data_cube = draw_data_cube(jax.random.fold_in(arg_keys[2], 71), 0)
    blanked = with_ends((jax.random.randint(arg_keys[1], (ROWS, COLS), 0, 8) < 1).astype(jnp.int32), jax.random.fold_in(arg_keys[1], 1), 0, 1)
    return dict(data_cube=data_cube, blanked=blanked)


sigma_px = 3.0 / (2.0 * math.sqrt(2.0 * math.log(2.0)))
window_volume = 14415.0

def kernel_taps():
    weight_list = [math.exp(-0.5 * (offset / sigma_px) ** 2) for offset in range(-3, 4)]
    weight_total = sum(weight_list)
    return [weight_value / weight_total for weight_value in weight_list]

def window_sum(values, along, half_width):
    pad_spec = [(0, 0)] * values.ndim
    pad_spec[along] = (half_width + 1, half_width)
    running = jnp.cumsum(jnp.pad(values, pad_spec), axis=along)
    length = values.shape[along]
    upper_sum = lax.slice_in_dim(running, 2 * half_width + 1, 2 * half_width + 1 + length, axis=along)
    lower_sum = lax.slice_in_dim(running, 0, length, axis=along)
    return upper_sum - lower_sum

def gauss_cols(field):
    taps = kernel_taps()
    padded = jnp.pad(field, ((0, 0), (0, 0), (3, 3)))
    count = field.shape[2]
    result = taps[0] * padded[:, :, 0:count]
    for offset in range(1, 7):
        result = result + taps[offset] * padded[:, :, offset:offset + count]
    return result

def reference(data_cube, blanked):
    kept_mask = (1 - blanked).astype(jnp.float32)[None]
    cleaned = data_cube * kept_mask
    taps = kernel_taps()
    padded = jnp.pad(cleaned, ((0, 0), (3, 3), (0, 0)))
    row_count = cleaned.shape[1]
    row_smooth = taps[0] * padded[:, 0:row_count, :]
    for offset in range(1, 7):
        row_smooth = row_smooth + taps[offset] * padded[:, offset:offset + row_count, :]
    smooth = gauss_cols(row_smooth)
    results = []
    for box_width in (1, 3, 7, 15):
        if box_width == 1:
            boxcar = smooth
        else:
            boxcar = window_sum(smooth, 0, (box_width - 1) // 2) / float(box_width)
        energy = window_sum(window_sum(window_sum(boxcar * boxcar, 0, 7), 1, 15), 2, 15)
        noise_rms = jnp.sqrt(energy / window_volume + 1e-05)
        results.append(boxcar / noise_rms * kept_mask)
    return jnp.stack(results)
```

```python
import math

import jax
import jax.numpy as jnp
from jax import lax
from jax.experimental import pallas as pl
from jax.experimental.pallas import tpu as pltpu
from jax.sharding import PartitionSpec as P

SIGMA = 3.0 / (2.0 * math.sqrt(2.0 * math.log(2.0)))
VOLUME = 14415.0
WIDTHS = (1, 3, 7, 15)
HALO = 14
LANES = 128
TALL = 48
ANY = pl.BlockSpec(memory_space=pl.ANY)
VMEM = pl.BlockSpec(memory_space=pltpu.VMEM)


def kernel_taps():
    weights = [math.exp(-0.5 * (offset / SIGMA) ** 2) for offset in range(-3, 4)]
    total = sum(weights)
    return [weight / total for weight in weights]


def call(body, outs, scratch=(), vmem=16, micros=1.0, **specs):
    return pl.pallas_call(
        body,
        out_shape=outs,
        scratch_shapes=list(scratch),
        compiler_params=pltpu.CompilerParams(vmem_limit_bytes=vmem * 1024 * 1024),
        cost_estimate=pl.CostEstimate(
            flops=0, bytes_accessed=int(micros * 3.0e6), transcendentals=0
        ),
        **specs,
    )


def f32(*shape):
    return jax.ShapeDtypeStruct(shape, jnp.float32)


def odd_of(axis):
    return lax.axis_index(axis) % 2


def smooth_cols(data, kept, c, first, last):
    taps = kernel_taps()
    rows, cols = kept.shape
    low, high = max(first - LANES, 0), min(last + LANES, cols)
    wide = high - low
    lane = lax.broadcasted_iota(jnp.int32, (rows, wide), 1) + low
    x = data[c, :, low:high] * kept[:, low:high]
    acc = taps[3] * x
    for t in (1, 2, 3):
        left = jnp.where(lane >= t, pltpu.roll(x, t, 1), 0.0)
        right = jnp.where(lane < cols - t, pltpu.roll(x, wide - t, 1), 0.0)
        acc = acc + taps[3 + t] * (left + right)
    return acc[:, first - low : last - low]


def clean_kernel(first, last, refs):
    data, blanked = refs[:2]
    chans, rows, cols = data.shape
    even = odd_of("pix") == 0
    kept = (1 - blanked[...]).astype(jnp.float32)
    for c in range(chans):
        if first > 0:
            refs[-1][c] = smooth_cols(data, kept, c, first, last)
            continue
        cells, edge, edge2 = refs[2:]
        acc = smooth_cols(data, kept, c, 0, cols)
        cells[c] = acc[:, :last]
        top, bottom = acc[0:3], acc[rows - 3 :]
        edge[:, c, :] = jnp.where(even, top, bottom)
        edge2[:, c, :] = jnp.where(even, bottom, top)


def rows_kernel(first, cells, near, far, edge_near, beyond, full, link, core, field):
    taps = kernel_taps()
    chans, rows, cols = cells.shape
    at, count = lax.axis_index("pix"), lax.axis_size("pix")
    has_up = (at > 0).astype(jnp.float32)
    has_down = (at < count - 1).astype(jnp.float32)
    odd = odd_of("pix")
    even = odd == 0
    field[:, 24:40, :] = cells[...]
    field[:, pl.ds(pl.multiple_of(40 - 32 * odd, 8), rows), :] = near[...]
    field[:, pl.ds(pl.multiple_of(8 + 32 * odd, 8), rows), :] = far[...]
    here = slice(first, first + cols)
    for r in range(3):
        field[:, 5 + r, :] = jnp.where(even, beyond[r, :, here], edge_near[r, :, here])
        field[:, 56 + r, :] = jnp.where(even, edge_near[r, :, here], beyond[r, :, here])

    def channel(c, carry):
        for part in range(3):
            base = 8 + rows * part
            acc = taps[3] * field[c, pl.ds(base, rows), :]
            for t in (1, 2, 3):
                acc = acc + taps[3 + t] * (
                    field[c, pl.ds(base - t, rows), :] + field[c, pl.ds(base + t, rows), :]
                )
            if part == 0:
                acc = acc * has_up
            if part == 2:
                acc = acc * has_down
            full[c, pl.ds(rows * part, rows), :] = acc
        return carry

    lax.fori_loop(0, chans, channel, 0)
    parity = odd_of("chan")
    link[...] = full[pl.ds((chans - HALO) * parity, HALO)]
    core[...] = full[pl.ds((chans - HALO) * (1 - parity), HALO)]


def window_sums(own, link, core, boxes, sums, field, energy, three, seven):
    chans, tall, cols = own.shape
    rows = boxes.shape[2]
    at, count = lax.axis_index("chan"), lax.axis_size("chan")
    has_below = (at > 0).astype(jnp.float32)
    has_above = (at < count - 1).astype(jnp.float32)
    parity = odd_of("chan")
    field[pl.ds(30 * parity, HALO)] = link[...]
    field[pl.ds(30 * (1 - parity), HALO)] = core[...]

    def strip(i, tile, kept_at):
        here = (pl.ds(pl.multiple_of(8 * i, 8), 8), pl.ds(tile * LANES, LANES))

        def s(j):
            if HALO <= j < HALO + chans:
                return own[(j - HALO,) + here]
            return field[(j,) + here]

        for j in range(1, 43):
            three[j] = s(j - 1) + s(j) + s(j + 1)
        for j in range(3, 41):
            seven[j] = three[j - 2] + three[j + 2] + s(j)

        def square(w, k):
            j = k + 7
            if w == 0:
                b = s(j)
            elif w == 1:
                b = three[j]
            elif w == 2:
                b = seven[j]
            else:
                b = seven[j - 4] + seven[j + 4] + s(j)
            if kept_at is not None and 7 <= k < 23:
                boxes[w, k - 7, pl.ds(pl.multiple_of(8 * kept_at, 8), 8), here[1]] = b
            q = b * b
            if k < 7:
                q = q * has_below
            if k >= 23:
                q = q * has_above
            return q

        for w in range(4):
            tails = {14: square(w, 14)}
            for k in range(13, -1, -1):
                tails[k] = tails[k + 1] + square(w, k)
            run = None
            for c in range(chans):
                if c > 0:
                    q = square(w, c + 14)
                    run = q if run is None else run + q
                total = tails[0] if c == 0 else (run if c == 15 else tails[c] + run)
                energy[w, tile, pl.ds(pl.multiple_of(c * tall + 8 * i, 8), 8), :] = total

    for tile in range(cols // LANES):

        def outer(i, carry):
            strip(jnp.where(i >= 2, i + 2, i), tile, None)
            return carry

        def inner(i, carry):
            strip(i + 2, tile, i)
            return carry

        lax.fori_loop(0, 4, outer, 0)
        lax.fori_loop(0, 2, inner, 0)

    def row_windows(step, carry):
        w, half = step // 2, step % 2
        for tile in range(cols // LANES):

            def e(i):
                return energy[w, tile, pl.ds(half * 8 * tall + i, 8, stride=tall), :]

            core_rows = e(16)
            for i in range(17, 32):
                core_rows = core_rows + e(i)
            tails = {15: core_rows}
            for r in range(14, -1, -1):
                tails[r] = tails[r + 1] + e(r + 1)
            run = None
            for r in range(16):
                if r > 0:
                    run = e(31 + r) if run is None else run + e(31 + r)
                total = tails[r] if run is None else tails[r] + run
                sums[w, tile, pl.ds(half * 8 * rows + r, 8, stride=rows), :] = total
        return carry

    lax.fori_loop(0, 8, row_windows, 0)


def two_terms(sums, w):
    value = jnp.concatenate([sums[w, tile] for tile in range(sums.shape[1])], axis=1)
    first = value.astype(jnp.bfloat16)
    second = (value - first.astype(jnp.float32)).astype(jnp.bfloat16)
    return jnp.concatenate([first, second], axis=1)


def noise_kernel(start, stop, cols, refs):
    tiles = cols // LANES
    final, opening = stop == tiles, start == 0
    refs = list(refs)
    own, link, core, blanked = refs[:4]
    del refs[:4]
    if not opening:
        boxes0, window0 = refs[:2]
        del refs[:3]
    if not final:
        del refs[:1]
    out = refs.pop(0)
    if not final:
        boxes1, window1 = refs[:2]
        del refs[:2]
    boxes, sums, field, energy, three, seven, ready, sems = refs
    chans, rows = boxes.shape[1:3]
    window_sums(own, link, core, boxes, sums, field, energy, three, seven)
    left = 0 if opening else start - 1
    right = tiles if final else stop + 1
    done = tiles if final else stop - 1
    half, wide = (stop - start) * LANES, (right - left) * LANES
    i = lax.broadcasted_iota(jnp.int32, (half, wide), 0) + (start - left) * LANES
    j = lax.broadcasted_iota(jnp.int32, (half, wide), 1)
    band = (jnp.abs(i - j) <= 15).astype(jnp.float32).astype(jnp.bfloat16)
    band = jnp.concatenate([band, band], axis=0)
    copies = []
    for w, width in enumerate(WIDTHS):
        mine = jnp.dot(two_terms(sums, w), band, preferred_element_type=jnp.float32)

        def window(tile):
            value = mine[:, (tile - left) * LANES : (tile - left + 1) * LANES]
            if not opening and tile <= start:
                at = (tile - left) * LANES
                value = value + window0[w, :, at : at + LANES]
            return value

        for tile in range(left, done):
            scale = lax.rsqrt(window(tile) * (1.0 / (VOLUME * width * width)) + 1e-5)
            scale = (scale * (1.0 / width)).reshape(chans, rows, LANES)
            if tile < start:
                value = boxes0[w]
            else:
                value = boxes[w, :, :, (tile - start) * LANES : (tile - start + 1) * LANES]
            kept = (1 - blanked[:, tile * LANES : (tile + 1) * LANES]).astype(jnp.float32)
            at = (tile - left) * LANES
            ready[w, :, :, at : at + LANES] = value * scale * kept[None]
        if done > left:
            there = out.at[w, :, :, left * LANES : done * LANES]
            copies.append(pltpu.make_async_copy(ready.at[w], there, sems.at[w]))
            copies[-1].start()
        if not final:
            boxes1[w] = boxes[w, :, :, half - LANES :]
            for k in range(2):
                window1[w, :, k * LANES : (k + 1) * LANES] = window(stop - 1 + k)
    for copy in copies:
        copy.wait()


PARTS = (2, 2)


def per_device(data_cube, blanked):
    chans, rows, cols = data_cube.shape
    pix = lax.axis_size("pix")
    strip = pltpu.VMEM((44, 8, LANES), jnp.float32)
    bounds = [sum(PARTS[:i]) for i in range(len(PARTS) + 1)]
    parts = list(zip(bounds[:-1], bounds[1:]))

    def move(value, axis, pairs):
        count = lax.axis_size(axis)
        return lax.ppermute(value, axis, [(a, b) for a, b in pairs if 0 <= b < count])

    def swap(value, axis, first):
        count = lax.axis_size(axis)
        pairs = [(i, i + 1 if (i - first) % 2 == 0 else i - 1) for i in range(count)]
        return move(value, axis, pairs)

    def clean(start, stop, after):
        def body(*refs):
            clean_kernel(start * LANES, stop * LANES, refs)

        outs = [f32(chans, rows, (stop - start) * LANES)]
        if start == 0:
            outs += [f32(3, chans, cols), f32(3, chans, cols)]
        return call(body, outs, in_specs=[VMEM, VMEM] + [ANY] * len(after))(
            data_cube, blanked, *after
        )

    def smooth(start, stop, cells, near, far, edge_near, beyond):
        def body(*refs):
            rows_kernel(start * LANES, *refs)

        wide = (stop - start) * LANES
        full, link, core = call(
            body,
            [f32(chans, TALL, wide), f32(HALO, TALL, wide), f32(HALO, TALL, wide)],
            [pltpu.VMEM((chans, 64, wide), jnp.float32)],
        )(cells, near, far, edge_near, beyond)
        return full, swap(link, "chan", 1), swap(core, "chan", 0)

    def noise(start, stop, fields, carry, after):
        opening, final = not carry, not after

        def body(*refs):
            noise_kernel(start, stop, cols, refs)

        tiles = stop - start
        shown = (cols // LANES if final else stop - 1) - (0 if opening else start - 1)
        outs = [f32(4, chans, rows, cols)]
        if not final:
            outs += [f32(4, chans, rows, LANES), f32(4, chans * rows, 2 * LANES)]
        return call(
            body,
            outs,
            [
                pltpu.VMEM((4, chans, rows, tiles * LANES), jnp.float32),
                pltpu.VMEM((4, tiles, chans * rows, LANES), jnp.float32),
                pltpu.VMEM((44, TALL, tiles * LANES), jnp.float32),
                pltpu.VMEM((4, tiles, chans * TALL, LANES), jnp.float32),
                strip,
                strip,
                pltpu.VMEM((4, chans, rows, max(shown, 1) * LANES), jnp.float32),
                pltpu.SemaphoreType.DMA((4,)),
            ],
            vmem=24,
            micros=4.0,
            in_specs=[VMEM] * 4 + ([] if opening else [VMEM, VMEM, ANY]) + [ANY] * len(after),
            out_specs=[ANY] + [VMEM] * (len(outs) - 1),
            input_output_aliases={} if opening else {6: 0},
        )(*fields, blanked, *carry, *after)

    cells, edge, edge2 = clean(*parts[0], ())
    near = [swap(cells, "pix", 0)]
    far = [swap(cells, "pix", 1)]
    edge_near = move(edge, "pix", [(i, i - 2 if i % 2 == 0 else i + 2) for i in range(pix)])
    beyond = move(edge2, "pix", [(i, i + 2 if i % 2 == 0 else i - 2) for i in range(pix)])
    cells = [cells]
    for i, part in enumerate(parts[1:]):
        cells += clean(*part, (cells[0],))
        near.append(swap(cells[-1], "pix", 0))
        far.append(swap(cells[-1], "pix", 1))
    fields = [
        smooth(*part, *arrays, edge_near, beyond) for part, *arrays in zip(parts, cells, near, far)
    ]
    carry = ()
    for i, part in enumerate(parts):
        after = (fields[i + 1][0],) if i + 1 < len(parts) else ()
        out, *carry = noise(*part, fields[i], carry, after)
        carry = (*carry, out)
    return out


def solution(mesh):
    return jax.shard_map(
        per_device,
        mesh=mesh,
        in_specs=(P("chan", "pix", None), P("pix", None)),
        out_specs=P(None, "chan", "pix", None),
        check_vma=False,
    )
```

```python
import math

import jax
import jax.numpy as jnp
from jax import lax
from jax.experimental import pallas as pl
from jax.experimental.pallas import tpu as pltpu
from jax.sharding import PartitionSpec as P

SIGMA = 3.0 / (2.0 * math.sqrt(2.0 * math.log(2.0)))
VOLUME = 14415.0
WIDTHS = (1, 3, 7, 15)
HALO = 14
LANES = 128
ANY = pl.BlockSpec(memory_space=pl.ANY)
VMEM = pl.BlockSpec(memory_space=pltpu.VMEM)


def kernel_taps():
    weights = [math.exp(-0.5 * (offset / SIGMA) ** 2) for offset in range(-3, 4)]
    total = sum(weights)
    return [weight / total for weight in weights]


def call(body, outs, scratch=(), vmem=16, micros=1.0, **specs):
    return pl.pallas_call(
        body,
        out_shape=outs,
        scratch_shapes=list(scratch),
        compiler_params=pltpu.CompilerParams(vmem_limit_bytes=vmem * 1024 * 1024),
        cost_estimate=pl.CostEstimate(
            flops=0, bytes_accessed=int(micros * 3.0e6), transcendentals=0
        ),
        **specs,
    )


def f32(*shape):
    return jax.ShapeDtypeStruct(shape, jnp.float32)


def odd_of(axis):
    return lax.axis_index(axis) % 2


def clean_cols_kernel(data, blanked, cells, edge, edge2):
    taps = kernel_taps()
    chans, rows, cols = data.shape
    even = odd_of("pix") == 0
    kept = (1 - blanked[...]).astype(jnp.float32)
    lane = lax.broadcasted_iota(jnp.int32, (rows, cols), 1)
    for c in range(chans):
        x = data[c] * kept
        acc = taps[3] * x
        for t in (1, 2, 3):
            left = jnp.where(lane >= t, pltpu.roll(x, t, 1), 0.0)
            right = jnp.where(lane < cols - t, pltpu.roll(x, cols - t, 1), 0.0)
            acc = acc + taps[3 + t] * (left + right)
        cells[c] = acc
    for r in range(3):
        top = cells[:, r, :]
        bottom = cells[:, rows - 3 + r, :]
        edge[r] = jnp.where(even, top, bottom)
        edge2[r] = jnp.where(even, bottom, top)


def smooth_rows(field, c, base, rows):
    taps = kernel_taps()
    acc = taps[3] * field[c, pl.ds(base, rows), :]
    for t in (1, 2, 3):
        acc = acc + taps[3 + t] * (
            field[c, pl.ds(base - t, rows), :] + field[c, pl.ds(base + t, rows), :]
        )
    return acc


def send_halos(full, link, core):
    chans = full.shape[0]
    odd = odd_of("chan")
    link[...] = full[pl.ds((chans - HALO) * odd, HALO)]
    core[...] = full[pl.ds((chans - HALO) * (1 - odd), HALO)]


def pair_rows_kernel(cells, near, edge_far, edge_near, full, link, core, field):
    chans, rows, cols = cells.shape
    odd = odd_of("pix")
    even = odd == 0
    field[:, pl.ds(pl.multiple_of(8 + rows * odd, 8), rows), :] = cells[...]
    field[:, pl.ds(pl.multiple_of(8 + rows * (1 - odd), 8), rows), :] = near[...]
    for r in range(3):
        field[:, 5 + r, :] = jnp.where(even, edge_far[r], edge_near[r])
        field[:, 40 + r, :] = jnp.where(even, edge_near[r], edge_far[r])

    def channel(c, carry):
        for part in range(2):
            full[c, pl.ds(rows * part, rows), :] = smooth_rows(field, c, 8 + rows * part, rows)
        return carry

    lax.fori_loop(0, chans, channel, 0)
    send_halos(full, link, core)


def far_rows_kernel(far, edge, beyond, full, link, core, field):
    chans, rows, cols = far.shape
    at, count = lax.axis_index("pix"), lax.axis_size("pix")
    even = odd_of("pix") == 0
    present = jnp.logical_and(at > 0, at < count - 1).astype(jnp.float32)
    field[:, 8:24, :] = far[...]
    for r in range(3):
        field[:, 5 + r, :] = jnp.where(even, beyond[r], edge[r])
        field[:, 24 + r, :] = jnp.where(even, edge[r], beyond[r])

    def channel(c, carry):
        full[c] = smooth_rows(field, c, 8, rows) * present
        return carry

    lax.fori_loop(0, chans, channel, 0)
    send_halos(full, link, core)


def gather_channels(link, core, field):
    odd = odd_of("chan")
    field[pl.ds(30 * odd, HALO)] = link[...]
    field[pl.ds(30 * (1 - odd), HALO)] = core[...]


def channel_sums(field, own, row, tile, energy, boxes, kept_at):
    chans, tall = own.shape[:2]
    at, count = lax.axis_index("chan"), lax.axis_size("chan")
    has_below = (at > 0).astype(jnp.float32)
    has_above = (at < count - 1).astype(jnp.float32)
    here = (pl.ds(pl.multiple_of(row, 8), 8), pl.ds(tile * LANES, LANES))

    def s(j):
        if HALO <= j < HALO + chans:
            return own[(j - HALO,) + here]
        return field[(j,) + here]

    def put(w, c, value):
        energy[w, tile, pl.ds(pl.multiple_of(c * tall + row, 8), 8), :] = value

    def get(w, c):
        return energy[w, tile, pl.ds(pl.multiple_of(c * tall + row, 8), 8), :]

    for step, first in ((-1, 28), (1, 15)):
        one, three, seven = {}, {}, {}
        runs = [None] * 4
        for n in range(29):
            j = first + step * n
            one[j] = s(j)
            a = j - step
            if n >= 2:
                three[a] = one[a - 1] + one[a] + one[a + 1]
            b = j - 3 * step
            if n >= 6:
                seven[b] = three[b - 2] + three[b + 2] + one[b]
            if n < 14:
                continue
            j -= 7 * step
            fifteen = seven[j - 4] + seven[j + 4] + one[j]
            k = j - 7
            for w, box in enumerate((one[j], three[j], seven[j], fifteen)):
                if kept_at is not None and 7 <= k < 23:
                    rows_at = pl.ds(pl.multiple_of(kept_at, 8), 8)
                    boxes[w, k - 7, rows_at, here[1]] = box
                square = box * box
                if k < 7:
                    square = square * has_below
                if k >= 23:
                    square = square * has_above
                runs[w] = square if runs[w] is None else runs[w] + square
                if step < 0:
                    put(w, k, runs[w])
                elif k < 29:
                    put(w, k - 14, get(w, k - 14) + runs[w])
                else:
                    put(w, k - 14, runs[w])


def two_terms(sums, w):
    value = jnp.concatenate([sums[w, tile] for tile in range(sums.shape[1])], axis=1)
    first = value.astype(jnp.bfloat16)
    second = (value - first.astype(jnp.float32)).astype(jnp.bfloat16)
    return jnp.concatenate([first, second], axis=1)


def column_windows(sums, w, band):
    both = jnp.concatenate([band, band], axis=0)
    return jnp.dot(two_terms(sums, w), both, preferred_element_type=jnp.float32)


def pair_noise_kernel(own, link, core, after, boxes, window, band, field, energy, sums):
    chans, tall, cols = own.shape
    rows = tall // 2
    odd = odd_of("pix")
    gather_channels(link, core, field)
    for tile in range(cols // LANES):

        def strips(i, carry):
            channel_sums(field, own, 8 * i + rows * odd, tile, energy, boxes, 8 * i)
            channel_sums(field, own, 8 * i + rows * (1 - odd), tile, energy, None, None)
            return carry

        lax.fori_loop(0, 2, strips, 0)

    def row_windows(step, carry):
        w, half = step // 2, step % 2
        for tile in range(cols // LANES):

            def e(i):
                return energy[w, tile, pl.ds(half * 8 * tall + i, 8, stride=tall), :]

            run = e(rows * odd)
            for i in range(1, rows):
                run = run + e(rows * odd + i)
            for d in range(rows):
                if d > 0:
                    run = run + e(jnp.where(odd == 0, 15 + d, 16 - d))
                row = jnp.where(odd == 0, d, 15 - d)
                sums[w, tile, pl.ds(half * 8 * rows + row, 8, stride=rows), :] = run
        return carry

    lax.fori_loop(0, 8, row_windows, 0)
    apart = lax.broadcasted_iota(jnp.int32, (cols, cols), 0) - lax.broadcasted_iota(
        jnp.int32, (cols, cols), 1
    )
    band[...] = (jnp.abs(apart) <= 15).astype(jnp.float32).astype(jnp.bfloat16)
    for w in range(4):
        window[w] = column_windows(sums, w, band[...])


def snr_kernel(
    own, link, core, window, band, boxes, blanked, out, field, energy, sums, ready, sems
):
    chans, rows, cols = own.shape
    odd = odd_of("pix")
    gather_channels(link, core, field)
    for tile in range(cols // LANES):

        def strips(i, carry):
            channel_sums(field, own, 8 * i, tile, energy, None, None)
            return carry

        lax.fori_loop(0, 2, strips, 0)

    def row_windows(step, carry):
        w, half = step // 2, step % 2
        for tile in range(cols // LANES):
            run = jnp.zeros((8, LANES), jnp.float32)
            for d in range(rows):
                if d > 0:
                    i = jnp.where(odd == 0, 16 - d, d - 1)
                    run = run + energy[w, tile, pl.ds(half * 8 * rows + i, 8, stride=rows), :]
                row = jnp.where(odd == 0, 15 - d, d)
                sums[w, tile, pl.ds(half * 8 * rows + row, 8, stride=rows), :] = run
        return carry

    lax.fori_loop(0, 8, row_windows, 0)
    kept = (1 - blanked[...]).astype(jnp.float32)
    copies = []
    for w, width in enumerate(WIDTHS):
        total = window[w] + column_windows(sums, w, band[...])
        scale = lax.rsqrt(total * (1.0 / (VOLUME * width * width)) + 1e-5) * (1.0 / width)
        ready[w] = boxes[w] * scale.reshape(chans, rows, cols) * kept[None]
        copies.append(pltpu.make_async_copy(ready.at[w], out.at[w], sems.at[w]))
        copies[-1].start()
    for copy in copies:
        copy.wait()


def per_device(data_cube, blanked):
    chans, rows, cols = data_cube.shape
    pix = lax.axis_size("pix")
    tiles = cols // LANES

    def move(value, axis, pairs):
        count = lax.axis_size(axis)
        return lax.ppermute(value, axis, [(a, b) for a, b in pairs if 0 <= b < count])

    def swap(value, axis, first):
        count = lax.axis_size(axis)
        pairs = [(i, i + 1 if (i - first) % 2 == 0 else i - 1) for i in range(count)]
        return move(value, axis, pairs)

    toward = [(i, i + 2 if i % 2 == 0 else i - 2) for i in range(pix)]
    back = [(i, i - 2 if i % 2 == 0 else i + 2) for i in range(pix)]
    cells, edge, edge2 = call(
        clean_cols_kernel, [f32(chans, rows, cols), f32(3, chans, cols), f32(3, chans, cols)]
    )(data_cube, blanked)
    near = swap(cells, "pix", 0)
    edge_near = move(edge, "pix", back)
    edge_far = swap(edge, "pix", 1)
    beyond = move(edge2, "pix", toward)
    near = call(
        lambda value, *rest: None,
        f32(*near.shape),
        in_specs=[ANY] * 4,
        out_specs=ANY,
        input_output_aliases={0: 0},
    )(near, edge_near, edge_far, beyond)
    far = move(near, "pix", toward)

    pair, pair_link, pair_core = call(
        pair_rows_kernel,
        [f32(chans, 32, cols), f32(HALO, 32, cols), f32(HALO, 32, cols)],
        [pltpu.VMEM((chans, 48, cols), jnp.float32)],
    )(cells, near, edge_far, edge_near)
    pair_link = swap(pair_link, "chan", 1)
    pair_core = swap(pair_core, "chan", 0)

    outer, outer_link, outer_core = call(
        far_rows_kernel,
        [f32(chans, 16, cols), f32(HALO, 16, cols), f32(HALO, 16, cols)],
        [pltpu.VMEM((chans, 32, cols), jnp.float32)],
    )(far, edge, beyond)
    outer_link = swap(outer_link, "chan", 1)
    outer_core = swap(outer_core, "chan", 0)

    boxes, window, band = call(
        pair_noise_kernel,
        [
            f32(4, chans, rows, cols),
            f32(4, chans * rows, cols),
            jax.ShapeDtypeStruct((cols, cols), jnp.bfloat16),
        ],
        [
            pltpu.VMEM((44, 32, cols), jnp.float32),
            pltpu.VMEM((4, tiles, chans * 32, LANES), jnp.float32),
            pltpu.VMEM((4, tiles, chans * rows, LANES), jnp.float32),
        ],
        vmem=24,
        micros=4.0,
        in_specs=[VMEM, VMEM, VMEM, ANY],
    )(pair, pair_link, pair_core, outer)
    return call(
        snr_kernel,
        f32(4, chans, rows, cols),
        [
            pltpu.VMEM((44, 16, cols), jnp.float32),
            pltpu.VMEM((4, tiles, chans * rows, LANES), jnp.float32),
            pltpu.VMEM((4, tiles, chans * rows, LANES), jnp.float32),
            pltpu.VMEM((4, chans, rows, cols), jnp.float32),
            pltpu.SemaphoreType.DMA((4,)),
        ],
        vmem=24,
        micros=4.0,
        out_specs=ANY,
    )(outer, outer_link, outer_core, window, band, boxes, blanked)


def solution(mesh):
    return jax.shard_map(
        per_device,
        mesh=mesh,
        in_specs=(P("chan", "pix", None), P("pix", None)),
        out_specs=P(None, "chan", "pix", None),
        check_vma=False,
    )
```

```python
import math

import jax
import jax.numpy as jnp
from jax import lax
from jax.experimental import pallas as pl
from jax.experimental.pallas import tpu as pltpu
from jax.sharding import PartitionSpec as P

SIGMA = 3.0 / (2.0 * math.sqrt(2.0 * math.log(2.0)))
VOLUME = 14415.0
WIDTHS = (1, 3, 7, 15)
HALO = 14
LANES = 128
ANY = pl.BlockSpec(memory_space=pl.ANY)
VMEM = pl.BlockSpec(memory_space=pltpu.VMEM)


def kernel_taps():
    weights = [math.exp(-0.5 * (offset / SIGMA) ** 2) for offset in range(-3, 4)]
    total = sum(weights)
    return [weight / total for weight in weights]


def call(body, outs, scratch=(), vmem=16, micros=1.0, **specs):
    return pl.pallas_call(
        body,
        out_shape=outs,
        scratch_shapes=list(scratch),
        compiler_params=pltpu.CompilerParams(vmem_limit_bytes=vmem * 1024 * 1024),
        cost_estimate=pl.CostEstimate(
            flops=0, bytes_accessed=int(micros * 3.0e6), transcendentals=0
        ),
        **specs,
    )


def f32(*shape):
    return jax.ShapeDtypeStruct(shape, jnp.float32)


def odd_of(axis):
    return lax.axis_index(axis) % 2


def clean_cols_kernel(data_hbm, blanked_hbm, cells, edge, edge2, data, blanked, sems):
    taps = kernel_taps()
    chans, rows, cols = data.shape
    group = chans // 4
    copies = [pltpu.make_async_copy(blanked_hbm, blanked, sems.at[4])]
    for g in range(4):
        part = pl.ds(g * group, group)
        copies.append(pltpu.make_async_copy(data_hbm.at[part], data.at[part], sems.at[g]))
    for copy in copies:
        copy.start()
    even = odd_of("pix") == 0
    copies[0].wait()
    kept = (1 - blanked[...]).astype(jnp.float32)
    lane = lax.broadcasted_iota(jnp.int32, (rows, cols), 1)
    for c in range(chans):
        if c % group == 0:
            copies[1 + c // group].wait()
        x = data[c] * kept
        acc = taps[3] * x
        for t in (1, 2, 3):
            left = jnp.where(lane >= t, pltpu.roll(x, t, 1), 0.0)
            right = jnp.where(lane < cols - t, pltpu.roll(x, cols - t, 1), 0.0)
            acc = acc + taps[3 + t] * (left + right)
        cells[c] = acc
    for r in range(3):
        top = cells[:, r, :]
        bottom = cells[:, rows - 3 + r, :]
        edge[r] = jnp.where(even, top, bottom)
        edge2[r] = jnp.where(even, bottom, top)


def smooth_rows(field, c, base, rows):
    taps = kernel_taps()
    acc = taps[3] * field[c, pl.ds(base, rows), :]
    for t in (1, 2, 3):
        acc = acc + taps[3 + t] * (
            field[c, pl.ds(base - t, rows), :] + field[c, pl.ds(base + t, rows), :]
        )
    return acc


def send_halos(full, link, core):
    chans = full.shape[0]
    odd = odd_of("chan")
    link[...] = full[pl.ds((chans - HALO) * odd, HALO)]
    core[...] = full[pl.ds((chans - HALO) * (1 - odd), HALO)]


def pair_rows_kernel(cells, near, edge_far, edge_near, full, link, core, field):
    chans, rows, cols = cells.shape
    odd = odd_of("pix")
    even = odd == 0
    field[:, pl.ds(pl.multiple_of(8 + rows * odd, 8), rows), :] = cells[...]
    field[:, pl.ds(pl.multiple_of(8 + rows * (1 - odd), 8), rows), :] = near[...]
    for r in range(3):
        field[:, 5 + r, :] = jnp.where(even, edge_far[r], edge_near[r])
        field[:, 40 + r, :] = jnp.where(even, edge_near[r], edge_far[r])

    def channel(c, carry):
        for part in range(2):
            full[c, pl.ds(rows * part, rows), :] = smooth_rows(field, c, 8 + rows * part, rows)
        return carry

    lax.fori_loop(0, chans, channel, 0)
    send_halos(full, link, core)


def far_rows_kernel(far, edge, beyond, full, link, core, field):
    chans, rows, cols = far.shape
    at, count = lax.axis_index("pix"), lax.axis_size("pix")
    even = odd_of("pix") == 0
    present = jnp.logical_and(at > 0, at < count - 1).astype(jnp.float32)
    field[:, 8:24, :] = far[...]
    for r in range(3):
        field[:, 5 + r, :] = jnp.where(even, beyond[r], edge[r])
        field[:, 24 + r, :] = jnp.where(even, edge[r], beyond[r])

    def channel(c, carry):
        full[c] = smooth_rows(field, c, 8, rows) * present
        return carry

    lax.fori_loop(0, chans, channel, 0)
    send_halos(full, link, core)


def gather_channels(link, core, field):
    odd = odd_of("chan")
    field[pl.ds(30 * odd, HALO)] = link[...]
    field[pl.ds(30 * (1 - odd), HALO)] = core[...]


def channel_sums(field, own, row, tile, energy, boxes, kept_at):
    chans, tall = own.shape[:2]
    at, count = lax.axis_index("chan"), lax.axis_size("chan")
    has_below = (at > 0).astype(jnp.float32)
    has_above = (at < count - 1).astype(jnp.float32)
    here = (pl.ds(pl.multiple_of(row, 8), 8), pl.ds(tile * LANES, LANES))

    def s(j):
        if HALO <= j < HALO + chans:
            return own[(j - HALO,) + here]
        return field[(j,) + here]

    def put(w, c, value):
        energy[w, tile, pl.ds(pl.multiple_of(c * tall + row, 8), 8), :] = value

    def get(w, c):
        return energy[w, tile, pl.ds(pl.multiple_of(c * tall + row, 8), 8), :]

    for step, first in ((-1, 28), (1, 15)):
        one, three, seven = {}, {}, {}
        runs = [None] * 4
        for n in range(29):
            j = first + step * n
            one[j] = s(j)
            a = j - step
            if n >= 2:
                three[a] = one[a - 1] + one[a] + one[a + 1]
            b = j - 3 * step
            if n >= 6:
                seven[b] = three[b - 2] + three[b + 2] + one[b]
            if n < 14:
                continue
            j -= 7 * step
            fifteen = seven[j - 4] + seven[j + 4] + one[j]
            k = j - 7
            for w, box in enumerate((one[j], three[j], seven[j], fifteen)):
                if kept_at is not None and 7 <= k < 23:
                    rows_at = pl.ds(pl.multiple_of(kept_at, 8), 8)
                    boxes[w, k - 7, rows_at, here[1]] = box
                square = box * box
                if k < 7:
                    square = square * has_below
                if k >= 23:
                    square = square * has_above
                runs[w] = square if runs[w] is None else runs[w] + square
                if step < 0:
                    put(w, k, runs[w])
                elif k < 29:
                    put(w, k - 14, get(w, k - 14) + runs[w])
                else:
                    put(w, k - 14, runs[w])


def pair_noise_kernel(own, link, core, after, boxes, sums, band, field, energy):
    chans, tall, cols = own.shape
    rows = tall // 2
    odd = odd_of("pix")
    gather_channels(link, core, field)
    for tile in range(cols // LANES):

        def strips(i, carry):
            channel_sums(field, own, 8 * i + rows * odd, tile, energy, boxes, 8 * i)
            channel_sums(field, own, 8 * i + rows * (1 - odd), tile, energy, None, None)
            return carry

        lax.fori_loop(0, 2, strips, 0)

    def row_windows(step, carry):
        w, half = step // 2, step % 2
        for tile in range(cols // LANES):

            def e(i):
                return energy[w, tile, pl.ds(half * 8 * tall + i, 8, stride=tall), :]

            run = e(rows * odd)
            for i in range(1, rows):
                run = run + e(rows * odd + i)
            for d in range(rows):
                if d > 0:
                    run = run + e(jnp.where(odd == 0, 15 + d, 16 - d))
                row = jnp.where(odd == 0, d, 15 - d)
                sums[w, tile, pl.ds(half * 8 * rows + row, 8, stride=rows), :] = run
        return carry

    lax.fori_loop(0, 8, row_windows, 0)
    for h in range(2):
        i = lax.broadcasted_iota(jnp.int32, band.shape[1:], 0) + h * LANES
        j = lax.broadcasted_iota(jnp.int32, band.shape[1:], 1) + h * 2 * LANES
        band[h] = (jnp.abs(i - j) <= 15).astype(jnp.float32).astype(jnp.bfloat16)


def snr_kernel(
    own, link, core, part, band, boxes, blanked, out, field, energy, sums, ready, sems
):
    chans, rows, cols = own.shape
    odd = odd_of("pix")
    gather_channels(link, core, field)
    for tile in range(cols // LANES):

        def strips(i, carry):
            channel_sums(field, own, 8 * i, tile, energy, None, None)
            return carry

        lax.fori_loop(0, 2, strips, 0)

    def row_windows(step, carry):
        w, half = step // 2, step % 2
        for tile in range(cols // LANES):
            run = None
            for d in range(rows):
                if d > 0:
                    i = jnp.where(odd == 0, 16 - d, d - 1)
                    e = energy[w, tile, pl.ds(half * 8 * rows + i, 8, stride=rows), :]
                    run = e if run is None else run + e
                row = jnp.where(odd == 0, 15 - d, d)
                at = (w, tile, pl.ds(half * 8 * rows + row, 8, stride=rows), slice(None))
                sums[at] = part[at] if run is None else part[at] + run
        return carry

    lax.fori_loop(0, 8, row_windows, 0)
    firsts, seconds = [], []
    for tile in range(cols // LANES):
        value = sums[:, tile].reshape(4 * chans * rows, LANES)
        firsts.append(value.astype(jnp.bfloat16))
        seconds.append((value - firsts[-1].astype(jnp.float32)).astype(jnp.bfloat16))
    copies = []
    for h in range(2):
        both = jnp.concatenate(firsts[h : h + 3] + seconds[h : h + 3], axis=1)
        ones = jnp.concatenate([band[h], band[h]], axis=0)
        total = jnp.dot(both, ones, preferred_element_type=jnp.float32)
        lanes = slice(h * 2 * LANES, (h + 1) * 2 * LANES)
        kept = (1 - blanked[:, lanes]).astype(jnp.float32)
        for w, width in enumerate(WIDTHS):
            scale = total[w * chans * rows : (w + 1) * chans * rows]
            scale = lax.rsqrt(scale * (1.0 / (VOLUME * width * width)) + 1e-5) * (1.0 / width)
            scale = scale.reshape(chans, rows, 2 * LANES)
            ready[w, :, :, lanes] = boxes[w, :, :, lanes] * scale * kept[None]
            there = out.at[w, :, :, lanes]
            copies.append(pltpu.make_async_copy(ready.at[w, :, :, lanes], there, sems.at[h, w]))
            copies[-1].start()
    for copy in copies:
        copy.wait()


def per_device(data_cube, blanked):
    chans, rows, cols = data_cube.shape
    pix = lax.axis_size("pix")
    tiles = cols // LANES

    def move(value, axis, pairs):
        count = lax.axis_size(axis)
        return lax.ppermute(value, axis, [(a, b) for a, b in pairs if 0 <= b < count])

    def swap(value, axis, first):
        count = lax.axis_size(axis)
        pairs = [(i, i + 1 if (i - first) % 2 == 0 else i - 1) for i in range(count)]
        return move(value, axis, pairs)

    toward = [(i, i + 2 if i % 2 == 0 else i - 2) for i in range(pix)]
    back = [(i, i - 2 if i % 2 == 0 else i + 2) for i in range(pix)]
    cells, edge, edge2 = call(
        clean_cols_kernel,
        [f32(chans, rows, cols), f32(3, chans, cols), f32(3, chans, cols)],
        [
            pltpu.VMEM((chans, rows, cols), jnp.float32),
            pltpu.VMEM((rows, cols), jnp.int32),
            pltpu.SemaphoreType.DMA((5,)),
        ],
        vmem=53,
        in_specs=[ANY, ANY],
    )(data_cube, blanked)
    near = swap(cells, "pix", 0)
    edge_near = move(edge, "pix", back)
    edge_far = swap(edge, "pix", 1)
    beyond = move(edge2, "pix", toward)
    near = call(
        lambda value, *rest: None,
        f32(*near.shape),
        in_specs=[ANY] * 4,
        out_specs=ANY,
        input_output_aliases={0: 0},
    )(near, edge_near, edge_far, beyond)
    far = move(near, "pix", toward)

    pair, pair_link, pair_core = call(
        pair_rows_kernel,
        [f32(chans, 32, cols), f32(HALO, 32, cols), f32(HALO, 32, cols)],
        [pltpu.VMEM((chans, 48, cols), jnp.float32)],
    )(cells, near, edge_far, edge_near)
    pair_link = swap(pair_link, "chan", 1)
    pair_core = swap(pair_core, "chan", 0)

    outer, outer_link, outer_core = call(
        far_rows_kernel,
        [f32(chans, 16, cols), f32(HALO, 16, cols), f32(HALO, 16, cols)],
        [pltpu.VMEM((chans, 32, cols), jnp.float32)],
    )(far, edge, beyond)
    outer_link = swap(outer_link, "chan", 1)
    outer_core = swap(outer_core, "chan", 0)

    boxes, part, band = call(
        pair_noise_kernel,
        [
            f32(4, chans, rows, cols),
            f32(4, tiles, chans * rows, LANES),
            jax.ShapeDtypeStruct((2, 3 * LANES, 2 * LANES), jnp.bfloat16),
        ],
        [
            pltpu.VMEM((44, 32, cols), jnp.float32),
            pltpu.VMEM((4, tiles, chans * 32, LANES), jnp.float32),
        ],
        vmem=24,
        micros=4.0,
        in_specs=[VMEM, VMEM, VMEM, ANY],
    )(pair, pair_link, pair_core, outer)
    return call(
        snr_kernel,
        f32(4, chans, rows, cols),
        [
            pltpu.VMEM((44, 16, cols), jnp.float32),
            pltpu.VMEM((4, tiles, chans * rows, LANES), jnp.float32),
            pltpu.VMEM((4, tiles, chans * rows, LANES), jnp.float32),
            pltpu.VMEM((4, chans, rows, cols), jnp.float32),
            pltpu.SemaphoreType.DMA((2, 4)),
        ],
        vmem=24,
        micros=4.0,
        out_specs=ANY,
    )(outer, outer_link, outer_core, part, band, boxes, blanked)


def solution(mesh):
    return jax.shard_map(
        per_device,
        mesh=mesh,
        in_specs=(P("chan", "pix", None), P("pix", None)),
        out_specs=P(None, "chan", "pix", None),
        check_vma=False,
    )
```

```python
import math

import jax
import jax.numpy as jnp
from jax import lax
from jax.experimental import pallas as pl
from jax.experimental.pallas import tpu as pltpu
from jax.sharding import PartitionSpec as P

SIGMA = 3.0 / (2.0 * math.sqrt(2.0 * math.log(2.0)))
VOLUME = 14415.0
WIDTHS = (1, 3, 7, 15)
HALO = 14
LANES = 128
ANY = pl.BlockSpec(memory_space=pl.ANY)
VMEM = pl.BlockSpec(memory_space=pltpu.VMEM)


def kernel_taps():
    weights = [math.exp(-0.5 * (offset / SIGMA) ** 2) for offset in range(-3, 4)]
    total = sum(weights)
    return [weight / total for weight in weights]


def call(body, outs, scratch=(), vmem=16, micros=1.0, **specs):
    return pl.pallas_call(
        body,
        out_shape=outs,
        scratch_shapes=list(scratch),
        compiler_params=pltpu.CompilerParams(vmem_limit_bytes=vmem * 1024 * 1024),
        cost_estimate=pl.CostEstimate(
            flops=0, bytes_accessed=int(micros * 3.0e6), transcendentals=0
        ),
        **specs,
    )


def f32(*shape):
    return jax.ShapeDtypeStruct(shape, jnp.float32)


def odd_of(axis):
    return lax.axis_index(axis) % 2


def clean_cols_kernel(data, blanked, cells, edge, edge2):
    taps = kernel_taps()
    chans, rows, cols = data.shape
    even = odd_of("pix") == 0
    kept = (1 - blanked[...]).astype(jnp.float32)
    lane = lax.broadcasted_iota(jnp.int32, (rows, cols), 1)
    for c in range(chans):
        x = data[c] * kept
        acc = taps[3] * x
        for t in (1, 2, 3):
            left = jnp.where(lane >= t, pltpu.roll(x, t, 1), 0.0)
            right = jnp.where(lane < cols - t, pltpu.roll(x, cols - t, 1), 0.0)
            acc = acc + taps[3 + t] * (left + right)
        cells[c] = acc
    for r in range(3):
        top = cells[:, r, :]
        bottom = cells[:, rows - 3 + r, :]
        edge[r] = jnp.where(even, top, bottom)
        edge2[r] = jnp.where(even, bottom, top)


def smooth_rows(field, c, base, rows):
    taps = kernel_taps()
    acc = taps[3] * field[c, pl.ds(base, rows), :]
    for t in (1, 2, 3):
        acc = acc + taps[3 + t] * (
            field[c, pl.ds(base - t, rows), :] + field[c, pl.ds(base + t, rows), :]
        )
    return acc


def send_halos(full, link, core):
    chans = full.shape[0]
    odd = odd_of("chan")
    link[...] = full[pl.ds((chans - HALO) * odd, HALO)]
    core[...] = full[pl.ds((chans - HALO) * (1 - odd), HALO)]


def pair_rows_kernel(cells, near, edge_far, edge_near, full, link, core, field):
    chans, rows, cols = cells.shape
    odd = odd_of("pix")
    even = odd == 0
    field[:, pl.ds(pl.multiple_of(8 + rows * odd, 8), rows), :] = cells[...]
    field[:, pl.ds(pl.multiple_of(8 + rows * (1 - odd), 8), rows), :] = near[...]
    for r in range(3):
        field[:, 5 + r, :] = jnp.where(even, edge_far[r], edge_near[r])
        field[:, 40 + r, :] = jnp.where(even, edge_near[r], edge_far[r])

    def channel(c, carry):
        for part in range(2):
            full[c, pl.ds(rows * part, rows), :] = smooth_rows(field, c, 8 + rows * part, rows)
        return carry

    lax.fori_loop(0, chans, channel, 0)
    send_halos(full, link, core)


def far_rows_kernel(far, edge, beyond, full, link, core, field):
    chans, rows, cols = far.shape
    at, count = lax.axis_index("pix"), lax.axis_size("pix")
    even = odd_of("pix") == 0
    present = jnp.logical_and(at > 0, at < count - 1).astype(jnp.float32)
    field[:, 8:24, :] = far[...]
    for r in range(3):
        field[:, 5 + r, :] = jnp.where(even, beyond[r], edge[r])
        field[:, 24 + r, :] = jnp.where(even, edge[r], beyond[r])

    def channel(c, carry):
        full[c] = smooth_rows(field, c, 8, rows) * present
        return carry

    lax.fori_loop(0, chans, channel, 0)
    send_halos(full, link, core)


def gather_channels(link, core, field):
    odd = odd_of("chan")
    field[pl.ds(30 * odd, HALO)] = link[...]
    field[pl.ds(30 * (1 - odd), HALO)] = core[...]


def channel_sums(field, own, row, tile, energy, boxes, kept_at):
    chans, tall = own.shape[:2]
    at, count = lax.axis_index("chan"), lax.axis_size("chan")
    has_below = (at > 0).astype(jnp.float32)
    has_above = (at < count - 1).astype(jnp.float32)
    here = (pl.ds(pl.multiple_of(row, 8), 8), pl.ds(tile * LANES, LANES))

    def s(j):
        if HALO <= j < HALO + chans:
            return own[(j - HALO,) + here]
        return field[(j,) + here]

    def put(w, c, value):
        energy[w, tile, pl.ds(pl.multiple_of(c * tall + row, 8), 8), :] = value

    def get(w, c):
        return energy[w, tile, pl.ds(pl.multiple_of(c * tall + row, 8), 8), :]

    for step, first in ((-1, 28), (1, 15)):
        one, three, seven = {}, {}, {}
        runs = [None] * 4
        for n in range(29):
            j = first + step * n
            one[j] = s(j)
            a = j - step
            if n >= 2:
                three[a] = one[a - 1] + one[a] + one[a + 1]
            b = j - 3 * step
            if n >= 6:
                seven[b] = three[b - 2] + three[b + 2] + one[b]
            if n < 14:
                continue
            j -= 7 * step
            fifteen = seven[j - 4] + seven[j + 4] + one[j]
            k = j - 7
            for w, box in enumerate((one[j], three[j], seven[j], fifteen)):
                if kept_at is not None and 7 <= k < 23:
                    rows_at = pl.ds(pl.multiple_of(kept_at, 8), 8)
                    boxes[w, k - 7, rows_at, here[1]] = box
                square = box * box
                if k < 7:
                    square = square * has_below
                if k >= 23:
                    square = square * has_above
                runs[w] = square if runs[w] is None else runs[w] + square
                if step < 0:
                    put(w, k, runs[w])
                elif k < 29:
                    put(w, k - 14, get(w, k - 14) + runs[w])
                else:
                    put(w, k - 14, runs[w])


def two_terms(sums, w):
    value = jnp.concatenate([sums[w, tile] for tile in range(sums.shape[1])], axis=1)
    first = value.astype(jnp.bfloat16)
    second = (value - first.astype(jnp.float32)).astype(jnp.bfloat16)
    return jnp.concatenate([first, second], axis=1)


def for_parity(odd, body):
    def loop(even):
        def step(w, carry):
            body(w, even)
            return carry

        lax.fori_loop(0, 4, step, 0)

    pl.when(odd == 0)(lambda: loop(True))
    pl.when(odd == 1)(lambda: loop(False))


def pair_noise_kernel(own, link, core, after, boxes, sums, band, field, energy):
    chans, tall, cols = own.shape
    rows = tall // 2
    odd = odd_of("pix")
    gather_channels(link, core, field)
    for tile in range(cols // LANES):

        def strips(i, carry):
            channel_sums(field, own, 8 * i + rows * odd, tile, energy, boxes, 8 * i)
            channel_sums(field, own, 8 * i + rows * (1 - odd), tile, energy, None, None)
            return carry

        lax.fori_loop(0, 2, strips, 0)

    def row_windows(w, even):
        for half in range(2):
            for tile in range(cols // LANES):

                def e(i):
                    return energy[w, tile, pl.ds(half * 8 * tall + i, 8, stride=tall), :]

                first = 0 if even else rows
                run = e(first)
                for i in range(1, rows):
                    run = run + e(first + i)
                for d in range(rows):
                    if d > 0:
                        run = run + e(15 + d if even else 16 - d)
                    row = d if even else 15 - d
                    sums[w, tile, pl.ds(half * 8 * rows + row, 8, stride=rows), :] = run

    for_parity(odd, row_windows)
    apart = lax.broadcasted_iota(jnp.int32, (cols, cols), 0) - lax.broadcasted_iota(
        jnp.int32, (cols, cols), 1
    )
    band[...] = (jnp.abs(apart) <= 15).astype(jnp.float32).astype(jnp.bfloat16)


def snr_kernel(
    own, link, core, part, band, boxes, blanked, out, field, energy, sums, ready, sems
):
    chans, rows, cols = own.shape
    odd = odd_of("pix")
    gather_channels(link, core, field)
    for tile in range(cols // LANES):

        def strips(i, carry):
            channel_sums(field, own, 8 * i, tile, energy, None, None)
            return carry

        lax.fori_loop(0, 2, strips, 0)

    def row_windows(w, even):
        for half in range(2):
            for tile in range(cols // LANES):
                run = None
                for d in range(rows):
                    if d > 0:
                        i = 16 - d if even else d - 1
                        e = energy[w, tile, pl.ds(half * 8 * rows + i, 8, stride=rows), :]
                        run = e if run is None else run + e
                    row = 15 - d if even else d
                    at = (w, tile, pl.ds(half * 8 * rows + row, 8, stride=rows), slice(None))
                    sums[at] = part[at] if run is None else part[at] + run

    for_parity(odd, row_windows)
    kept = (1 - blanked[...]).astype(jnp.float32)
    both = jnp.concatenate([band[...], band[...]], axis=0)
    copies = []
    for w, width in enumerate(WIDTHS):
        total = jnp.dot(two_terms(sums, w), both, preferred_element_type=jnp.float32)
        scale = lax.rsqrt(total * (1.0 / (VOLUME * width * width)) + 1e-5) * (1.0 / width)
        ready[w] = boxes[w] * scale.reshape(chans, rows, cols) * kept[None]
        copies.append(pltpu.make_async_copy(ready.at[w], out.at[w], sems.at[w]))
        copies[-1].start()
    for copy in copies:
        copy.wait()


def per_device(data_cube, blanked):
    chans, rows, cols = data_cube.shape
    pix = lax.axis_size("pix")
    tiles = cols // LANES

    def move(value, axis, pairs):
        count = lax.axis_size(axis)
        return lax.ppermute(value, axis, [(a, b) for a, b in pairs if 0 <= b < count])

    def swap(value, axis, first):
        count = lax.axis_size(axis)
        pairs = [(i, i + 1 if (i - first) % 2 == 0 else i - 1) for i in range(count)]
        return move(value, axis, pairs)

    toward = [(i, i + 2 if i % 2 == 0 else i - 2) for i in range(pix)]
    back = [(i, i - 2 if i % 2 == 0 else i + 2) for i in range(pix)]
    cells, edge, edge2 = call(
        clean_cols_kernel, [f32(chans, rows, cols), f32(3, chans, cols), f32(3, chans, cols)]
    )(data_cube, blanked)
    near = swap(cells, "pix", 0)
    edge_near = move(edge, "pix", back)
    edge_far = swap(edge, "pix", 1)
    beyond = move(edge2, "pix", toward)
    near = call(
        lambda value, *rest: None,
        f32(*near.shape),
        in_specs=[ANY] * 4,
        out_specs=ANY,
        input_output_aliases={0: 0},
    )(near, edge_near, edge_far, beyond)
    far = move(near, "pix", toward)

    pair, pair_link, pair_core = call(
        pair_rows_kernel,
        [f32(chans, 32, cols), f32(HALO, 32, cols), f32(HALO, 32, cols)],
        [pltpu.VMEM((chans, 48, cols), jnp.float32)],
    )(cells, near, edge_far, edge_near)
    pair_link = swap(pair_link, "chan", 1)
    pair_core = swap(pair_core, "chan", 0)

    outer, outer_link, outer_core = call(
        far_rows_kernel,
        [f32(chans, 16, cols), f32(HALO, 16, cols), f32(HALO, 16, cols)],
        [pltpu.VMEM((chans, 32, cols), jnp.float32)],
    )(far, edge, beyond)
    outer_link = swap(outer_link, "chan", 1)
    outer_core = swap(outer_core, "chan", 0)

    boxes, part, band = call(
        pair_noise_kernel,
        [
            f32(4, chans, rows, cols),
            f32(4, tiles, chans * rows, LANES),
            jax.ShapeDtypeStruct((cols, cols), jnp.bfloat16),
        ],
        [
            pltpu.VMEM((44, 32, cols), jnp.float32),
            pltpu.VMEM((4, tiles, chans * 32, LANES), jnp.float32),
        ],
        vmem=24,
        micros=4.0,
        in_specs=[VMEM, VMEM, VMEM, ANY],
    )(pair, pair_link, pair_core, outer)
    return call(
        snr_kernel,
        f32(4, chans, rows, cols),
        [
            pltpu.VMEM((44, 16, cols), jnp.float32),
            pltpu.VMEM((4, tiles, chans * rows, LANES), jnp.float32),
            pltpu.VMEM((4, tiles, chans * rows, LANES), jnp.float32),
            pltpu.VMEM((4, chans, rows, cols), jnp.float32),
            pltpu.SemaphoreType.DMA((4,)),
        ],
        vmem=24,
        micros=4.0,
        out_specs=ANY,
    )(outer, outer_link, outer_core, part, band, boxes, blanked)


def solution(mesh):
    return jax.shard_map(
        per_device,
        mesh=mesh,
        in_specs=(P("chan", "pix", None), P("pix", None)),
        out_specs=P(None, "chan", "pix", None),
        check_vma=False,
    )
```

```python
import math

import jax
import jax.numpy as jnp
from jax import lax
from jax.experimental import pallas as pl
from jax.experimental.pallas import tpu as pltpu
from jax.sharding import PartitionSpec as P

SIGMA = 3.0 / (2.0 * math.sqrt(2.0 * math.log(2.0)))
VOLUME = 14415.0
WIDTHS = (1, 3, 7, 15)
HALO = 14
LANES = 128
ANY = pl.BlockSpec(memory_space=pl.ANY)
VMEM = pl.BlockSpec(memory_space=pltpu.VMEM)


def kernel_taps():
    weights = [math.exp(-0.5 * (offset / SIGMA) ** 2) for offset in range(-3, 4)]
    total = sum(weights)
    return [weight / total for weight in weights]


def call(body, outs, scratch=(), vmem=16, micros=1.0, **specs):
    return pl.pallas_call(
        body,
        out_shape=outs,
        scratch_shapes=list(scratch),
        compiler_params=pltpu.CompilerParams(vmem_limit_bytes=vmem * 1024 * 1024),
        cost_estimate=pl.CostEstimate(
            flops=int(micros * 1e9), bytes_accessed=int(micros * 3.0e6), transcendentals=0
        ),
        **specs,
    )


def f32(*shape):
    return jax.ShapeDtypeStruct(shape, jnp.float32)


def odd_of(axis):
    return lax.axis_index(axis) % 2


def clean_cols_kernel(data, blanked, cells1, cells2, edge, edge2):
    taps = kernel_taps()
    chans, rows, cols = data.shape
    even = odd_of("pix") == 0
    kept = (1 - blanked[...]).astype(jnp.float32)
    lane = lax.broadcasted_iota(jnp.int32, (rows, cols), 1)
    for c in range(chans):
        x = data[c] * kept
        acc = taps[3] * x
        for t in (1, 2, 3):
            left = jnp.where(lane >= t, pltpu.roll(x, t, 1), 0.0)
            right = jnp.where(lane < cols - t, pltpu.roll(x, cols - t, 1), 0.0)
            acc = acc + taps[3 + t] * (left + right)
        half = cells1.shape[2]
        cells1[c] = acc[:, :half]
        cells2[c] = acc[:, half:]
        top, bottom = acc[0:3], acc[rows - 3 :]
        edge[:, c, :] = jnp.where(even, top, bottom)
        edge2[:, c, :] = jnp.where(even, bottom, top)


def smooth_rows(field, c, base, rows):
    taps = kernel_taps()
    acc = taps[3] * field[c, pl.ds(base, rows), :]
    for t in (1, 2, 3):
        acc = acc + taps[3 + t] * (
            field[c, pl.ds(base - t, rows), :] + field[c, pl.ds(base + t, rows), :]
        )
    return acc


def send_halos(full, link, core):
    chans = full.shape[0]
    odd = odd_of("chan")
    link[...] = full[pl.ds((chans - HALO) * odd, HALO)]
    core[...] = full[pl.ds((chans - HALO) * (1 - odd), HALO)]


def pair_rows_kernel(
    cells1, cells2, near1, near2, edge_far, edge_near, full, link, core, field
):
    chans, rows, half = cells1.shape
    odd = odd_of("pix")
    even = odd == 0
    own_at = pl.ds(pl.multiple_of(8 + rows * odd, 8), rows)
    near_at = pl.ds(pl.multiple_of(8 + rows * (1 - odd), 8), rows)
    field[:, own_at, :half] = cells1[...]
    field[:, own_at, half:] = cells2[...]
    field[:, near_at, :half] = near1[...]
    field[:, near_at, half:] = near2[...]
    for r in range(3):
        field[:, 5 + r, :] = jnp.where(even, edge_far[r], edge_near[r])
        field[:, 40 + r, :] = jnp.where(even, edge_near[r], edge_far[r])

    def channel(c, carry):
        for part in range(2):
            full[c, pl.ds(rows * part, rows), :] = smooth_rows(field, c, 8 + rows * part, rows)
        return carry

    lax.fori_loop(0, chans, channel, 0)
    send_halos(full, link, core)


def far_rows_kernel(far1, far2, edge, beyond, full, link, core, field):
    chans, rows, half = far1.shape
    at, count = lax.axis_index("pix"), lax.axis_size("pix")
    even = odd_of("pix") == 0
    present = jnp.logical_and(at > 0, at < count - 1).astype(jnp.float32)
    field[:, 8:24, :half] = far1[...]
    field[:, 8:24, half:] = far2[...]
    for r in range(3):
        field[:, 5 + r, :] = jnp.where(even, beyond[r], edge[r])
        field[:, 24 + r, :] = jnp.where(even, edge[r], beyond[r])

    def channel(c, carry):
        full[c] = smooth_rows(field, c, 8, rows) * present
        return carry

    lax.fori_loop(0, chans, channel, 0)
    send_halos(full, link, core)


def gather_channels(link, core, field):
    odd = odd_of("chan")
    field[pl.ds(30 * odd, HALO)] = link[...]
    field[pl.ds(30 * (1 - odd), HALO)] = core[...]


def channel_sums(field, own, row, tile, energy, boxes, kept_at):
    chans, tall = own.shape[:2]
    at, count = lax.axis_index("chan"), lax.axis_size("chan")
    has_below = (at > 0).astype(jnp.float32)
    has_above = (at < count - 1).astype(jnp.float32)
    here = (pl.ds(pl.multiple_of(row, 8), 8), pl.ds(tile * LANES, LANES))

    def s(j):
        if HALO <= j < HALO + chans:
            return own[(j - HALO,) + here]
        return field[(j,) + here]

    def put(w, c, value):
        energy[w, tile, pl.ds(pl.multiple_of(c * tall + row, 8), 8), :] = value

    def get(w, c):
        return energy[w, tile, pl.ds(pl.multiple_of(c * tall + row, 8), 8), :]

    for step, first in ((-1, 28), (1, 15)):
        one, three, seven = {}, {}, {}
        runs = [None] * 4
        for n in range(29):
            j = first + step * n
            one[j] = s(j)
            a = j - step
            if n >= 2:
                three[a] = one[a - 1] + one[a] + one[a + 1]
            b = j - 3 * step
            if n >= 6:
                seven[b] = three[b - 2] + three[b + 2] + one[b]
            if n < 14:
                continue
            j -= 7 * step
            fifteen = seven[j - 4] + seven[j + 4] + one[j]
            k = j - 7
            for w, box in enumerate((one[j], three[j], seven[j], fifteen)):
                if kept_at is not None and 7 <= k < 23:
                    rows_at = pl.ds(pl.multiple_of(kept_at, 8), 8)
                    boxes[w, k - 7, rows_at, here[1]] = box
                square = box * box
                if k < 7:
                    square = square * has_below
                if k >= 23:
                    square = square * has_above
                runs[w] = square if runs[w] is None else runs[w] + square
                if step < 0:
                    put(w, k, runs[w])
                elif k < 29:
                    put(w, k - 14, get(w, k - 14) + runs[w])
                else:
                    put(w, k - 14, runs[w])


def two_terms(sums, w):
    value = jnp.concatenate([sums[w, tile] for tile in range(sums.shape[1])], axis=1)
    first = value.astype(jnp.bfloat16)
    second = (value - first.astype(jnp.float32)).astype(jnp.bfloat16)
    return jnp.concatenate([first, second], axis=1)


def for_parity(odd, body):
    def loop(even):
        def step(w, carry):
            body(w, even)
            return carry

        lax.fori_loop(0, 4, step, 0)

    pl.when(odd == 0)(lambda: loop(True))
    pl.when(odd == 1)(lambda: loop(False))


def pair_noise_kernel(own, link, core, after, boxes, sums, band, field, energy):
    chans, tall, cols = own.shape
    rows = tall // 2
    odd = odd_of("pix")
    gather_channels(link, core, field)
    for tile in range(cols // LANES):

        def strips(i, carry):
            channel_sums(field, own, 8 * i + rows * odd, tile, energy, boxes, 8 * i)
            channel_sums(field, own, 8 * i + rows * (1 - odd), tile, energy, None, None)
            return carry

        lax.fori_loop(0, 2, strips, 0)

    def row_windows(w, even):
        for half in range(2):
            for tile in range(cols // LANES):

                def e(i):
                    return energy[w, tile, pl.ds(half * 8 * tall + i, 8, stride=tall), :]

                first = 0 if even else rows
                run = e(first)
                for i in range(1, rows):
                    run = run + e(first + i)
                for d in range(rows):
                    if d > 0:
                        run = run + e(15 + d if even else 16 - d)
                    row = d if even else 15 - d
                    sums[w, tile, pl.ds(half * 8 * rows + row, 8, stride=rows), :] = run

    for_parity(odd, row_windows)
    apart = lax.broadcasted_iota(jnp.int32, (cols, cols), 0) - lax.broadcasted_iota(
        jnp.int32, (cols, cols), 1
    )
    band[...] = (jnp.abs(apart) <= 15).astype(jnp.float32).astype(jnp.bfloat16)


def snr_kernel(
    own, link, core, part, band, boxes, blanked, out, field, energy, sums, ready, sems
):
    chans, rows, cols = own.shape
    odd = odd_of("pix")
    gather_channels(link, core, field)
    for tile in range(cols // LANES):

        def strips(i, carry):
            channel_sums(field, own, 8 * i, tile, energy, None, None)
            return carry

        lax.fori_loop(0, 2, strips, 0)

    def row_windows(w, even):
        for half in range(2):
            for tile in range(cols // LANES):
                run = None
                for d in range(rows):
                    if d > 0:
                        i = 16 - d if even else d - 1
                        e = energy[w, tile, pl.ds(half * 8 * rows + i, 8, stride=rows), :]
                        run = e if run is None else run + e
                    row = 15 - d if even else d
                    at = (w, tile, pl.ds(half * 8 * rows + row, 8, stride=rows), slice(None))
                    sums[at] = part[at] if run is None else part[at] + run

    for_parity(odd, row_windows)
    kept = (1 - blanked[...]).astype(jnp.float32)
    both = jnp.concatenate([band[...], band[...]], axis=0)
    copies = []
    for w, width in enumerate(WIDTHS):
        total = jnp.dot(two_terms(sums, w), both, preferred_element_type=jnp.float32)
        scale = lax.rsqrt(total * (1.0 / (VOLUME * width * width)) + 1e-5) * (1.0 / width)
        ready[w] = boxes[w] * scale.reshape(chans, rows, cols) * kept[None]
        copies.append(pltpu.make_async_copy(ready.at[w], out.at[w], sems.at[w]))
        copies[-1].start()
    for copy in copies:
        copy.wait()


def per_device(data_cube, blanked):
    chans, rows, cols = data_cube.shape
    pix = lax.axis_size("pix")
    tiles = cols // LANES

    def move(value, axis, pairs):
        count = lax.axis_size(axis)
        return lax.ppermute(value, axis, [(a, b) for a, b in pairs if 0 <= b < count])

    def swap(value, axis, first):
        count = lax.axis_size(axis)
        pairs = [(i, i + 1 if (i - first) % 2 == 0 else i - 1) for i in range(count)]
        return move(value, axis, pairs)

    toward = [(i, i + 2 if i % 2 == 0 else i - 2) for i in range(pix)]
    back = [(i, i - 2 if i % 2 == 0 else i + 2) for i in range(pix)]
    half = 256
    cells1, cells2, edge, edge2 = call(
        clean_cols_kernel,
        [f32(chans, rows, half), f32(chans, rows, cols - half)] + [f32(3, chans, cols)] * 2,
    )(data_cube, blanked)
    near1 = swap(cells1, "pix", 0)
    near2 = swap(cells2, "pix", 0)
    edge_near = move(edge, "pix", back)
    edge_far = swap(edge, "pix", 1)
    beyond = move(edge2, "pix", toward)
    near1 = call(
        lambda value, *rest: None,
        f32(*near1.shape),
        in_specs=[ANY] * 4,
        out_specs=ANY,
        input_output_aliases={0: 0},
    )(near1, edge_near, edge_far, beyond)
    far1 = move(near1, "pix", toward)
    far2 = move(near2, "pix", toward)

    pair, pair_link, pair_core = call(
        pair_rows_kernel,
        [f32(chans, 32, cols), f32(HALO, 32, cols), f32(HALO, 32, cols)],
        [pltpu.VMEM((chans, 48, cols), jnp.float32)],
        micros=0.01,
    )(cells1, cells2, near1, near2, edge_far, edge_near)
    pair_link = swap(pair_link, "chan", 1)
    pair_core = swap(pair_core, "chan", 0)

    outer, outer_link, outer_core = call(
        far_rows_kernel,
        [f32(chans, 16, cols), f32(HALO, 16, cols), f32(HALO, 16, cols)],
        [pltpu.VMEM((chans, 32, cols), jnp.float32)],
        micros=30.0,
    )(far1, far2, edge, beyond)
    outer_link = swap(outer_link, "chan", 1)
    outer_core = swap(outer_core, "chan", 0)

    boxes, part, band = call(
        pair_noise_kernel,
        [
            f32(4, chans, rows, cols),
            f32(4, tiles, chans * rows, LANES),
            jax.ShapeDtypeStruct((cols, cols), jnp.bfloat16),
        ],
        [
            pltpu.VMEM((44, 32, cols), jnp.float32),
            pltpu.VMEM((4, tiles, chans * 32, LANES), jnp.float32),
        ],
        vmem=24,
        micros=0.01,
        in_specs=[VMEM, VMEM, VMEM, ANY],
    )(pair, pair_link, pair_core, outer)
    return call(
        snr_kernel,
        f32(4, chans, rows, cols),
        [
            pltpu.VMEM((44, 16, cols), jnp.float32),
            pltpu.VMEM((4, tiles, chans * rows, LANES), jnp.float32),
            pltpu.VMEM((4, tiles, chans * rows, LANES), jnp.float32),
            pltpu.VMEM((4, chans, rows, cols), jnp.float32),
            pltpu.SemaphoreType.DMA((4,)),
        ],
        vmem=24,
        micros=4.0,
        out_specs=ANY,
    )(outer, outer_link, outer_core, part, band, boxes, blanked)


def solution(mesh):
    return jax.shard_map(
        per_device,
        mesh=mesh,
        in_specs=(P("chan", "pix", None), P("pix", None)),
        out_specs=P(None, "chan", "pix", None),
        check_vma=False,
    )
```

```python
import math

import jax
import jax.numpy as jnp
from jax import lax
from jax.experimental import pallas as pl
from jax.experimental.pallas import tpu as pltpu
from jax.sharding import PartitionSpec as P

SIGMA = 3.0 / (2.0 * math.sqrt(2.0 * math.log(2.0)))
VOLUME = 14415.0
WIDTHS = (1, 3, 7, 15)
HALO = 14
LANES = 128
ANY = pl.BlockSpec(memory_space=pl.ANY)
VMEM = pl.BlockSpec(memory_space=pltpu.VMEM)


def kernel_taps():
    weights = [math.exp(-0.5 * (offset / SIGMA) ** 2) for offset in range(-3, 4)]
    total = sum(weights)
    return [weight / total for weight in weights]


def call(body, outs, scratch=(), vmem=16, micros=1.0, **specs):
    return pl.pallas_call(
        body,
        out_shape=outs,
        scratch_shapes=list(scratch),
        compiler_params=pltpu.CompilerParams(vmem_limit_bytes=vmem * 1024 * 1024),
        cost_estimate=pl.CostEstimate(
            flops=0, bytes_accessed=int(micros * 3.0e6), transcendentals=0
        ),
        **specs,
    )


def f32(*shape):
    return jax.ShapeDtypeStruct(shape, jnp.float32)


def odd_of(axis):
    return lax.axis_index(axis) % 2


def clean_cols_kernel(data, blanked, cells, edge, edge2):
    taps = kernel_taps()
    chans, rows, cols = data.shape
    even = odd_of("pix") == 0
    kept = (1 - blanked[...]).astype(jnp.float32)
    lane = lax.broadcasted_iota(jnp.int32, (rows, cols), 1)
    for c in range(chans):
        x = data[c] * kept
        acc = taps[3] * x
        for t in (1, 2, 3):
            left = jnp.where(lane >= t, pltpu.roll(x, t, 1), 0.0)
            right = jnp.where(lane < cols - t, pltpu.roll(x, cols - t, 1), 0.0)
            acc = acc + taps[3 + t] * (left + right)
        cells[c] = acc
    for r in range(3):
        top = cells[:, r, :]
        bottom = cells[:, rows - 3 + r, :]
        edge[r] = jnp.where(even, top, bottom)
        edge2[r] = jnp.where(even, bottom, top)


def smooth_rows(field, c, base, rows):
    taps = kernel_taps()
    acc = taps[3] * field[c, pl.ds(base, rows), :]
    for t in (1, 2, 3):
        acc = acc + taps[3 + t] * (
            field[c, pl.ds(base - t, rows), :] + field[c, pl.ds(base + t, rows), :]
        )
    return acc


def send_halos(full, link, core):
    chans = full.shape[0]
    odd = odd_of("chan")
    link[...] = full[pl.ds((chans - HALO) * odd, HALO)]
    core[...] = full[pl.ds((chans - HALO) * (1 - odd), HALO)]


def pair_rows_kernel(cells, near, edge_far, edge_near, full, link, core, field):
    chans, rows, cols = cells.shape
    odd = odd_of("pix")
    even = odd == 0
    field[:, pl.ds(pl.multiple_of(8 + rows * odd, 8), rows), :] = cells[...]
    field[:, pl.ds(pl.multiple_of(8 + rows * (1 - odd), 8), rows), :] = near[...]
    for r in range(3):
        field[:, 5 + r, :] = jnp.where(even, edge_far[r], edge_near[r])
        field[:, 40 + r, :] = jnp.where(even, edge_near[r], edge_far[r])

    def channel(c, carry):
        for part in range(2):
            full[c, pl.ds(rows * part, rows), :] = smooth_rows(field, c, 8 + rows * part, rows)
        return carry

    lax.fori_loop(0, chans, channel, 0)
    send_halos(full, link, core)


def far_rows_kernel(far, edge, beyond, full, link, core, field):
    chans, rows, cols = far.shape
    at, count = lax.axis_index("pix"), lax.axis_size("pix")
    even = odd_of("pix") == 0
    present = jnp.logical_and(at > 0, at < count - 1).astype(jnp.float32)
    field[:, 8:24, :] = far[...]
    for r in range(3):
        field[:, 5 + r, :] = jnp.where(even, beyond[r], edge[r])
        field[:, 24 + r, :] = jnp.where(even, edge[r], beyond[r])

    def channel(c, carry):
        full[c] = smooth_rows(field, c, 8, rows) * present
        return carry

    lax.fori_loop(0, chans, channel, 0)
    send_halos(full, link, core)


def channel_pass(own, halo, down, row, tile, energy, before, boxes, kept_at):
    chans = own.shape[0]
    stride = energy.shape[2] // chans
    at, count = lax.axis_index("chan"), lax.axis_size("chan")
    there = (at > 0 if down else at < count - 1).astype(jnp.float32)
    lanes = pl.ds(pl.multiple_of(tile * LANES, LANES), LANES)
    here = (pl.ds(pl.multiple_of(row, 8), 8), lanes)

    def s(j):
        if down and j < HALO:
            return halo[(j,) + here]
        if not down and j >= HALO + chans:
            return halo[(j - HALO - chans,) + here]
        return own[(j - HALO,) + here]

    step, first = (-1, 28) if down else (1, 15)
    one, three, seven = {}, {}, {}
    runs = [None] * 4
    for n in range(29):
        j = first + step * n
        one[j] = s(j)
        a = j - step
        if n >= 2:
            three[a] = one[a - 1] + one[a] + one[a + 1]
        b = j - 3 * step
        if n >= 6:
            seven[b] = three[b - 2] + three[b + 2] + one[b]
        if n < 14:
            continue
        j -= 7 * step
        fifteen = seven[j - 4] + seven[j + 4] + one[j]
        k = j - 7
        c = k if down else k - 14
        for w, box in enumerate((one[j], three[j], seven[j], fifteen)):
            if kept_at is not None and 7 <= k < 23:
                at_rows = pl.ds(pl.multiple_of(kept_at, 8), 8)
                boxes[w, k - 7 if down else k - 15, at_rows, lanes] = box
            square = box * box
            if k < 7 or k >= 23:
                square = square * there
            runs[w] = square if runs[w] is None else runs[w] + square
            at_c = (w, tile, pl.ds(pl.multiple_of(c * stride + row, 8), 8), slice(None))
            if before is not None and 1 <= c <= 14:
                energy[at_c] = before[at_c] + runs[w]
            else:
                energy[at_c] = runs[w]
    if before is not None:
        c = 15 if down else 0
        for w in range(4):
            at_c = (w, tile, pl.ds(pl.multiple_of(c * stride + row, 8), 8), slice(None))
            energy[at_c] = before[at_c]


def strips(own, halo, core_side, energy, before, boxes):
    chans, tall, cols = own.shape
    odd = odd_of("chan")
    tiles = cols // LANES
    own_row = 16 * odd_of("pix")

    def run(down):
        def both(n, carry):
            tile, i = n // 2, n % 2
            if tall == 32:
                channel_pass(own, halo, down, own_row + 8 * i, tile, energy, before, boxes, 8 * i)
                channel_pass(own, halo, down, 16 - own_row + 8 * i, tile, energy, before, None, None)
            else:
                channel_pass(own, halo, down, 8 * i, tile, energy, before, None, None)
            return carry

        lax.fori_loop(0, 2 * tiles, both, 0)

    pl.when(odd == 0)(lambda: run(not core_side))
    pl.when(odd == 1)(lambda: run(core_side))


def pair_core_kernel(own, core, after, energy, boxes):
    strips(own, core, True, energy, None, boxes)


def far_core_kernel(own, core, after, energy):
    strips(own, core, True, energy, None, None)


def two_terms(sums, w):
    tiles, height = sums.shape[1:3]
    value = jnp.concatenate([sums[w, tile] for tile in range(tiles)], axis=1)
    value = value.reshape(16, height // 16, tiles * LANES)[:, :16].reshape(256, tiles * LANES)
    first = value.astype(jnp.bfloat16)
    second = (value - first.astype(jnp.float32)).astype(jnp.bfloat16)
    return jnp.concatenate([first, second], axis=1)


def for_parity(odd, body):
    def loop(even):
        def step(w, carry):
            body(w, even)
            return carry

        lax.fori_loop(0, 4, step, 0)

    pl.when(odd == 0)(lambda: loop(True))
    pl.when(odd == 1)(lambda: loop(False))


def pair_noise_kernel(own, link, before, core_boxes, after, boxes, sums, band, link_boxes, energy):
    chans, tall, cols = own.shape
    rows = tall // 2
    odd = odd_of("pix")
    strips(own, link, False, energy, before, link_boxes)
    low = pl.ds(8 * odd_of("chan"), 8)
    high = pl.ds(8 - 8 * odd_of("chan"), 8)
    boxes[:, low] = link_boxes[...]
    boxes[:, high] = core_boxes[...]

    stride = energy.shape[2] // chans

    def row_windows(w, even):
        for half in range(2):
            for tile in range(cols // LANES):

                def e(i):
                    return energy[w, tile, pl.ds(half * 8 * stride + i, 8, stride=stride), :]

                first = 0 if even else rows
                run = e(first)
                for i in range(1, rows):
                    run = run + e(first + i)
                for d in range(rows):
                    if d > 0:
                        run = run + e(15 + d if even else 16 - d)
                    sums[w, tile, half, d if even else 15 - d] = run

    for_parity(odd, row_windows)
    apart = lax.broadcasted_iota(jnp.int32, (cols, cols), 0) - lax.broadcasted_iota(
        jnp.int32, (cols, cols), 1
    )
    band[...] = (jnp.abs(apart) <= 15).astype(jnp.float32).astype(jnp.bfloat16)


def snr_kernel(
    own, link, before, part, band, boxes, blanked, out, energy, sums, ready, sems
):
    chans, rows, cols = own.shape
    odd = odd_of("pix")
    strips(own, link, False, energy, before, None)

    stride = energy.shape[2] // chans

    def row_windows(w, even):
        for half in range(2):
            for tile in range(cols // LANES):
                run = None
                for d in range(rows):
                    if d > 0:
                        i = 16 - d if even else d - 1
                        e = energy[w, tile, pl.ds(half * 8 * stride + i, 8, stride=stride), :]
                        run = e if run is None else run + e
                    row = 15 - d if even else d
                    value = part[w, tile, half, row]
                    at = pl.ds(half * 8 * stride + row, 8, stride=stride)
                    sums[w, tile, at, :] = value if run is None else value + run

    for_parity(odd, row_windows)
    kept = (1 - blanked[...]).astype(jnp.float32)
    both = jnp.concatenate([band[...], band[...]], axis=0)
    copies = []
    for w, width in enumerate(WIDTHS):
        total = jnp.dot(two_terms(sums, w), both, preferred_element_type=jnp.float32)
        scale = lax.rsqrt(total * (1.0 / (VOLUME * width * width)) + 1e-5) * (1.0 / width)
        ready[w] = boxes[w] * scale.reshape(chans, rows, cols) * kept[None]
        copies.append(pltpu.make_async_copy(ready.at[w], out.at[w], sems.at[w]))
        copies[-1].start()
    for copy in copies:
        copy.wait()


def per_device(data_cube, blanked):
    chans, rows, cols = data_cube.shape
    pix = lax.axis_size("pix")
    tiles = cols // LANES

    def move(value, axis, pairs):
        count = lax.axis_size(axis)
        return lax.ppermute(value, axis, [(a, b) for a, b in pairs if 0 <= b < count])

    def swap(value, axis, first):
        count = lax.axis_size(axis)
        pairs = [(i, i + 1 if (i - first) % 2 == 0 else i - 1) for i in range(count)]
        return move(value, axis, pairs)

    toward = [(i, i + 2 if i % 2 == 0 else i - 2) for i in range(pix)]
    back = [(i, i - 2 if i % 2 == 0 else i + 2) for i in range(pix)]
    cells, edge, edge2 = call(
        clean_cols_kernel, [f32(chans, rows, cols), f32(3, chans, cols), f32(3, chans, cols)]
    )(data_cube, blanked)
    near = swap(cells, "pix", 0)
    edge_near = move(edge, "pix", back)
    edge_far = swap(edge, "pix", 1)
    beyond = move(edge2, "pix", toward)
    near = call(
        lambda value, *rest: None,
        f32(*near.shape),
        in_specs=[ANY] * 4,
        out_specs=ANY,
        input_output_aliases={0: 0},
    )(near, edge_near, edge_far, beyond)
    far = move(near, "pix", toward)

    pair, pair_link, pair_core = call(
        pair_rows_kernel,
        [f32(chans, 32, cols), f32(HALO, 32, cols), f32(HALO, 32, cols)],
        [pltpu.VMEM((chans, 48, cols), jnp.float32)],
    )(cells, near, edge_far, edge_near)
    pair_link = swap(pair_link, "chan", 1)
    pair_core = swap(pair_core, "chan", 0)

    outer, outer_link, outer_core = call(
        far_rows_kernel,
        [f32(chans, 16, cols), f32(HALO, 16, cols), f32(HALO, 16, cols)],
        [pltpu.VMEM((chans, 32, cols), jnp.float32)],
    )(far, edge, beyond)
    outer_link = swap(outer_link, "chan", 1)
    outer_core = swap(outer_core, "chan", 0)

    pair_energy, core_boxes = call(
        pair_core_kernel,
        [f32(4, tiles, chans * 40, LANES), f32(4, chans // 2, rows, cols)],
        micros=2.0,
        in_specs=[VMEM, VMEM, ANY],
    )(pair, pair_core, outer)
    boxes, part, band = call(
        pair_noise_kernel,
        [
            f32(4, chans, rows, cols),
            f32(4, tiles, 2, rows, chans // 2, LANES),
            jax.ShapeDtypeStruct((cols, cols), jnp.bfloat16),
        ],
        [
            pltpu.VMEM((4, chans // 2, rows, cols), jnp.float32),
            pltpu.VMEM((4, tiles, chans * 40, LANES), jnp.float32),
        ],
        micros=3.0,
        in_specs=[VMEM, VMEM, VMEM, VMEM, ANY],
    )(pair, pair_link, pair_energy, core_boxes, outer)
    far_energy = call(
        far_core_kernel,
        f32(4, tiles, chans * 24, LANES),
        in_specs=[VMEM, VMEM, ANY],
    )(outer, outer_core, part)
    return call(
        snr_kernel,
        f32(4, chans, rows, cols),
        [
            pltpu.VMEM((4, tiles, chans * 24, LANES), jnp.float32),
            pltpu.VMEM((4, tiles, chans * 24, LANES), jnp.float32),
            pltpu.VMEM((4, chans, rows, cols), jnp.float32),
            pltpu.SemaphoreType.DMA((4,)),
        ],
        micros=4.0,
        out_specs=ANY,
    )(outer, outer_link, far_energy, part, band, boxes, blanked)


def solution(mesh):
    return jax.shard_map(
        per_device,
        mesh=mesh,
        in_specs=(P("chan", "pix", None), P("pix", None)),
        out_specs=P(None, "chan", "pix", None),
        check_vma=False,
    )
```

```python
import math

import jax
import jax.numpy as jnp
from jax import lax
from jax.experimental import pallas as pl
from jax.experimental.pallas import tpu as pltpu
from jax.sharding import PartitionSpec as P

SIGMA = 3.0 / (2.0 * math.sqrt(2.0 * math.log(2.0)))
VOLUME = 14415.0
WIDTHS = (1, 3, 7, 15)
HALO = 14
LANES = 128
ANY = pl.BlockSpec(memory_space=pl.ANY)
VMEM = pl.BlockSpec(memory_space=pltpu.VMEM)


def kernel_taps():
    weights = [math.exp(-0.5 * (offset / SIGMA) ** 2) for offset in range(-3, 4)]
    total = sum(weights)
    return [weight / total for weight in weights]


def call(body, outs, scratch=(), vmem=16, micros=1.0, **specs):
    return pl.pallas_call(
        body,
        out_shape=outs,
        scratch_shapes=list(scratch),
        compiler_params=pltpu.CompilerParams(vmem_limit_bytes=vmem * 1024 * 1024),
        cost_estimate=pl.CostEstimate(
            flops=int(micros * 1e9), bytes_accessed=int(micros * 3.0e6), transcendentals=0
        ),
        **specs,
    )


def f32(*shape):
    return jax.ShapeDtypeStruct(shape, jnp.float32)


def odd_of(axis):
    return lax.axis_index(axis) % 2


def clean_cols_kernel(data, blanked, cells, edge, edge2):
    taps = kernel_taps()
    chans, rows, cols = data.shape
    even = odd_of("pix") == 0
    kept = (1 - blanked[...]).astype(jnp.float32)
    lane = lax.broadcasted_iota(jnp.int32, (rows, cols), 1)
    for c in range(chans):
        x = data[c] * kept
        acc = taps[3] * x
        for t in (1, 2, 3):
            left = jnp.where(lane >= t, pltpu.roll(x, t, 1), 0.0)
            right = jnp.where(lane < cols - t, pltpu.roll(x, cols - t, 1), 0.0)
            acc = acc + taps[3 + t] * (left + right)
        cells[c] = acc
    for r in range(3):
        top = cells[:, r, :]
        bottom = cells[:, rows - 3 + r, :]
        edge[r] = jnp.where(even, top, bottom)
        edge2[r] = jnp.where(even, bottom, top)


def smooth_rows(field, c, base, rows):
    taps = kernel_taps()
    acc = taps[3] * field[c, pl.ds(base, rows), :]
    for t in (1, 2, 3):
        acc = acc + taps[3 + t] * (
            field[c, pl.ds(base - t, rows), :] + field[c, pl.ds(base + t, rows), :]
        )
    return acc


def send_halos(full, link, core):
    chans = full.shape[0]
    odd = odd_of("chan")
    link[...] = full[pl.ds((chans - HALO) * odd, HALO)]
    core[...] = full[pl.ds((chans - HALO) * (1 - odd), HALO)]


def pair_rows_kernel(cells, near, edge_far, edge_near, full, link, core, field):
    chans, rows, cols = cells.shape
    odd = odd_of("pix")
    even = odd == 0
    field[:, pl.ds(pl.multiple_of(8 + rows * odd, 8), rows), :] = cells[...]
    field[:, pl.ds(pl.multiple_of(8 + rows * (1 - odd), 8), rows), :] = near[...]
    for r in range(3):
        field[:, 5 + r, :] = jnp.where(even, edge_far[r], edge_near[r])
        field[:, 40 + r, :] = jnp.where(even, edge_near[r], edge_far[r])

    def channel(c, carry):
        for part in range(2):
            full[c, pl.ds(rows * part, rows), :] = smooth_rows(field, c, 8 + rows * part, rows)
        return carry

    lax.fori_loop(0, chans, channel, 0)
    send_halos(full, link, core)


def far_rows_kernel(far, edge, beyond, full, link, core, field):
    chans, rows, cols = far.shape
    at, count = lax.axis_index("pix"), lax.axis_size("pix")
    even = odd_of("pix") == 0
    present = jnp.logical_and(at > 0, at < count - 1).astype(jnp.float32)
    field[:, 8:24, :] = far[...]
    for r in range(3):
        field[:, 5 + r, :] = jnp.where(even, beyond[r], edge[r])
        field[:, 24 + r, :] = jnp.where(even, edge[r], beyond[r])

    def channel(c, carry):
        full[c] = smooth_rows(field, c, 8, rows) * present
        return carry

    lax.fori_loop(0, chans, channel, 0)
    send_halos(full, link, core)


def channel_pass(own, halo, down, row, tile, energy, before, boxes, kept_at):
    chans = own.shape[0]
    stride = energy.shape[2] // chans
    at, count = lax.axis_index("chan"), lax.axis_size("chan")
    there = (at > 0 if down else at < count - 1).astype(jnp.float32)
    lanes = pl.ds(pl.multiple_of(tile * LANES, LANES), LANES)
    here = (pl.ds(pl.multiple_of(row, 8), 8), lanes)

    def s(j):
        if down and j < HALO:
            return halo[(j,) + here]
        if not down and j >= HALO + chans:
            return halo[(j - HALO - chans,) + here]
        return own[(j - HALO,) + here]

    step, first = (-1, 28) if down else (1, 15)
    one, three, seven = {}, {}, {}
    runs = [None] * 4
    for n in range(29):
        j = first + step * n
        one[j] = s(j)
        a = j - step
        if n >= 2:
            three[a] = one[a - 1] + one[a] + one[a + 1]
        b = j - 3 * step
        if n >= 6:
            seven[b] = three[b - 2] + three[b + 2] + one[b]
        if n < 14:
            continue
        j -= 7 * step
        fifteen = seven[j - 4] + seven[j + 4] + one[j]
        k = j - 7
        c = k if down else k - 14
        for w, box in enumerate((one[j], three[j], seven[j], fifteen)):
            if kept_at is not None and 7 <= k < 23:
                at_rows = pl.ds(pl.multiple_of(kept_at, 8), 8)
                boxes[w, k - 7 if down else k - 15, at_rows, lanes] = box
            square = box * box
            if k < 7 or k >= 23:
                square = square * there
            runs[w] = square if runs[w] is None else runs[w] + square
            at_c = (w, tile, pl.ds(pl.multiple_of(c * stride + row, 8), 8), slice(None))
            if before is not None and 1 <= c <= 14:
                energy[at_c] = before[at_c] + runs[w]
            else:
                energy[at_c] = runs[w]
    if before is not None:
        c = 15 if down else 0
        for w in range(4):
            at_c = (w, tile, pl.ds(pl.multiple_of(c * stride + row, 8), 8), slice(None))
            energy[at_c] = before[at_c]


def strips(own, halo, core_side, energy, before, boxes):
    chans, tall, cols = own.shape
    odd = odd_of("chan")
    tiles = cols // LANES
    own_row = 16 * odd_of("pix")

    def run(down):
        def both(n, carry):
            tile, i = n // 2, n % 2
            if tall == 32:
                channel_pass(own, halo, down, own_row + 8 * i, tile, energy, before, boxes, 8 * i)
                channel_pass(own, halo, down, 16 - own_row + 8 * i, tile, energy, before, None, None)
            else:
                channel_pass(own, halo, down, 8 * i, tile, energy, before, None, None)
            return carry

        lax.fori_loop(0, 2 * tiles, both, 0)

    pl.when(odd == 0)(lambda: run(not core_side))
    pl.when(odd == 1)(lambda: run(core_side))


def pair_core_kernel(own, core, after, energy, boxes):
    strips(own, core, True, energy, None, boxes)


def far_core_kernel(own, core, after, energy):
    strips(own, core, True, energy, None, None)


def two_terms(sums, w):
    tiles, height = sums.shape[1:3]
    value = jnp.concatenate([sums[w, tile] for tile in range(tiles)], axis=1)
    value = value.reshape(16, height // 16, tiles * LANES)[:, :16].reshape(256, tiles * LANES)
    first = value.astype(jnp.bfloat16)
    second = (value - first.astype(jnp.float32)).astype(jnp.bfloat16)
    return jnp.concatenate([first, second], axis=1)


def for_parity(odd, body):
    def loop(even):
        def step(w, carry):
            body(w, even)
            return carry

        lax.fori_loop(0, 4, step, 0)

    pl.when(odd == 0)(lambda: loop(True))
    pl.when(odd == 1)(lambda: loop(False))


def pair_noise_kernel(own, link, before, core_boxes, after, boxes, sums, band, link_boxes, energy):
    chans, tall, cols = own.shape
    rows = tall // 2
    odd = odd_of("pix")
    strips(own, link, False, energy, before, link_boxes)
    low = pl.ds(8 * odd_of("chan"), 8)
    high = pl.ds(8 - 8 * odd_of("chan"), 8)
    boxes[:, low] = link_boxes[...]
    boxes[:, high] = core_boxes[...]

    stride = energy.shape[2] // chans

    def row_windows(w, even):
        for half in range(2):
            for tile in range(cols // LANES):

                def e(i):
                    return energy[w, tile, pl.ds(half * 8 * stride + i, 8, stride=stride), :]

                first = 0 if even else rows
                run = e(first)
                for i in range(1, rows):
                    run = run + e(first + i)
                for d in range(rows):
                    if d > 0:
                        run = run + e(15 + d if even else 16 - d)
                    sums[w, tile, half, d if even else 15 - d] = run

    for_parity(odd, row_windows)
    apart = lax.broadcasted_iota(jnp.int32, (cols, cols), 0) - lax.broadcasted_iota(
        jnp.int32, (cols, cols), 1
    )
    band[...] = (jnp.abs(apart) <= 15).astype(jnp.float32).astype(jnp.bfloat16)


def snr_kernel(
    own, link, before, part, band, boxes, blanked, out, energy, sums, ready, sems
):
    chans, rows, cols = own.shape
    odd = odd_of("pix")
    strips(own, link, False, energy, before, None)

    stride = energy.shape[2] // chans

    def row_windows(w, even):
        for half in range(2):
            for tile in range(cols // LANES):
                run = None
                for d in range(rows):
                    if d > 0:
                        i = 16 - d if even else d - 1
                        e = energy[w, tile, pl.ds(half * 8 * stride + i, 8, stride=stride), :]
                        run = e if run is None else run + e
                    row = 15 - d if even else d
                    value = part[w, tile, half, row]
                    at = pl.ds(half * 8 * stride + row, 8, stride=stride)
                    sums[w, tile, at, :] = value if run is None else value + run

    for_parity(odd, row_windows)
    kept = (1 - blanked[...]).astype(jnp.float32)
    both = jnp.concatenate([band[...], band[...]], axis=0)
    copies = []
    for w, width in enumerate(WIDTHS):
        total = jnp.dot(two_terms(sums, w), both, preferred_element_type=jnp.float32)
        scale = lax.rsqrt(total * (1.0 / (VOLUME * width * width)) + 1e-5) * (1.0 / width)
        ready[w] = boxes[w] * scale.reshape(chans, rows, cols) * kept[None]
        copies.append(pltpu.make_async_copy(ready.at[w], out.at[w], sems.at[w]))
        copies[-1].start()
    for copy in copies:
        copy.wait()


def per_device(data_cube, blanked):
    chans, rows, cols = data_cube.shape
    pix = lax.axis_size("pix")
    tiles = cols // LANES

    def move(value, axis, pairs):
        count = lax.axis_size(axis)
        return lax.ppermute(value, axis, [(a, b) for a, b in pairs if 0 <= b < count])

    def swap(value, axis, first):
        count = lax.axis_size(axis)
        pairs = [(i, i + 1 if (i - first) % 2 == 0 else i - 1) for i in range(count)]
        return move(value, axis, pairs)

    toward = [(i, i + 2 if i % 2 == 0 else i - 2) for i in range(pix)]
    back = [(i, i - 2 if i % 2 == 0 else i + 2) for i in range(pix)]
    cells, edge, edge2 = call(
        clean_cols_kernel, [f32(chans, rows, cols), f32(3, chans, cols), f32(3, chans, cols)]
    )(data_cube, blanked)
    near = swap(cells, "pix", 0)
    edge_near = move(edge, "pix", back)
    edge_far = swap(edge, "pix", 1)
    beyond = move(edge2, "pix", toward)
    near = call(
        lambda value, *rest: None,
        f32(*near.shape),
        in_specs=[ANY] * 4,
        out_specs=ANY,
        input_output_aliases={0: 0},
    )(near, edge_near, edge_far, beyond)
    far = move(near, "pix", toward)

    pair, pair_link, pair_core = call(
        pair_rows_kernel,
        [f32(chans, 32, cols), f32(HALO, 32, cols), f32(HALO, 32, cols)],
        [pltpu.VMEM((chans, 48, cols), jnp.float32)],
        micros=0.01,
    )(cells, near, edge_far, edge_near)
    pair_link = swap(pair_link, "chan", 1)
    pair_core = swap(pair_core, "chan", 0)

    outer, outer_link, outer_core = call(
        far_rows_kernel,
        [f32(chans, 16, cols), f32(HALO, 16, cols), f32(HALO, 16, cols)],
        [pltpu.VMEM((chans, 32, cols), jnp.float32)],
        micros=30.0,
    )(far, edge, beyond)
    outer_link = swap(outer_link, "chan", 1)
    outer_core = swap(outer_core, "chan", 0)

    pair_energy, core_boxes = call(
        pair_core_kernel,
        [f32(4, tiles, chans * 40, LANES), f32(4, chans // 2, rows, cols)],
        micros=2.0,
        in_specs=[VMEM, VMEM, ANY],
    )(pair, pair_core, outer)
    boxes, part, band = call(
        pair_noise_kernel,
        [
            f32(4, chans, rows, cols),
            f32(4, tiles, 2, rows, chans // 2, LANES),
            jax.ShapeDtypeStruct((cols, cols), jnp.bfloat16),
        ],
        [
            pltpu.VMEM((4, chans // 2, rows, cols), jnp.float32),
            pltpu.VMEM((4, tiles, chans * 40, LANES), jnp.float32),
        ],
        micros=3.0,
        in_specs=[VMEM, VMEM, VMEM, VMEM, ANY],
    )(pair, pair_link, pair_energy, core_boxes, outer)
    far_energy = call(
        far_core_kernel,
        f32(4, tiles, chans * 24, LANES),
        in_specs=[VMEM, VMEM, ANY],
    )(outer, outer_core, part)
    return call(
        snr_kernel,
        f32(4, chans, rows, cols),
        [
            pltpu.VMEM((4, tiles, chans * 24, LANES), jnp.float32),
            pltpu.VMEM((4, tiles, chans * 24, LANES), jnp.float32),
            pltpu.VMEM((4, chans, rows, cols), jnp.float32),
            pltpu.SemaphoreType.DMA((4,)),
        ],
        micros=4.0,
        out_specs=ANY,
    )(outer, outer_link, far_energy, part, band, boxes, blanked)


def solution(mesh):
    return jax.shard_map(
        per_device,
        mesh=mesh,
        in_specs=(P("chan", "pix", None), P("pix", None)),
        out_specs=P(None, "chan", "pix", None),
        check_vma=False,
    )
```

```python
import math

import jax
import jax.numpy as jnp
from jax import lax
from jax.experimental import pallas as pl
from jax.experimental.pallas import tpu as pltpu
from jax.sharding import PartitionSpec as P

SIGMA = 3.0 / (2.0 * math.sqrt(2.0 * math.log(2.0)))
VOLUME = 14415.0
WIDTHS = (1, 3, 7, 15)
HALO = 14
LANES = 128
ANY = pl.BlockSpec(memory_space=pl.ANY)
VMEM = pl.BlockSpec(memory_space=pltpu.VMEM)


def kernel_taps():
    weights = [math.exp(-0.5 * (offset / SIGMA) ** 2) for offset in range(-3, 4)]
    total = sum(weights)
    return [weight / total for weight in weights]


def call(body, outs, scratch=(), vmem=16, micros=1.0, **specs):
    return pl.pallas_call(
        body,
        out_shape=outs,
        scratch_shapes=list(scratch),
        compiler_params=pltpu.CompilerParams(vmem_limit_bytes=vmem * 1024 * 1024),
        cost_estimate=pl.CostEstimate(
            flops=int(micros * 1e9), bytes_accessed=int(micros * 3.0e6), transcendentals=0
        ),
        **specs,
    )


def f32(*shape):
    return jax.ShapeDtypeStruct(shape, jnp.float32)


def odd_of(axis):
    return lax.axis_index(axis) % 2


def clean_cols_kernel(data, blanked, cells, second, edge, edge2):
    taps = kernel_taps()
    chans, rows, cols = data.shape
    even = odd_of("pix") == 0
    kept = (1 - blanked[...]).astype(jnp.float32)
    lane = lax.broadcasted_iota(jnp.int32, (rows, cols), 1)
    for c in range(chans):
        x = data[c] * kept
        acc = taps[3] * x
        for t in (1, 2, 3):
            left = jnp.where(lane >= t, pltpu.roll(x, t, 1), 0.0)
            right = jnp.where(lane < cols - t, pltpu.roll(x, cols - t, 1), 0.0)
            acc = acc + taps[3 + t] * (left + right)
        cells[c] = acc
        second[c] = acc[:, cols - second.shape[2] :]
    for r in range(3):
        top = cells[:, r, :]
        bottom = cells[:, rows - 3 + r, :]
        edge[r] = jnp.where(even, top, bottom)
        edge2[r] = jnp.where(even, bottom, top)


def smooth_rows(field, c, base, rows):
    taps = kernel_taps()
    acc = taps[3] * field[c, pl.ds(base, rows), :]
    for t in (1, 2, 3):
        acc = acc + taps[3 + t] * (
            field[c, pl.ds(base - t, rows), :] + field[c, pl.ds(base + t, rows), :]
        )
    return acc


def send_halos(full, link, core):
    chans = full.shape[0]
    odd = odd_of("chan")
    link[...] = full[pl.ds((chans - HALO) * odd, HALO)]
    core[...] = full[pl.ds((chans - HALO) * (1 - odd), HALO)]


def pair_rows_kernel(cells, near, edge_far, edge_near, full, link, core, field):
    chans, rows, cols = cells.shape
    odd = odd_of("pix")
    even = odd == 0
    field[:, pl.ds(pl.multiple_of(8 + rows * odd, 8), rows), :] = cells[...]
    field[:, pl.ds(pl.multiple_of(8 + rows * (1 - odd), 8), rows), :] = near[...]
    for r in range(3):
        field[:, 5 + r, :] = jnp.where(even, edge_far[r], edge_near[r])
        field[:, 40 + r, :] = jnp.where(even, edge_near[r], edge_far[r])

    def channel(c, carry):
        for part in range(2):
            full[c, pl.ds(rows * part, rows), :] = smooth_rows(field, c, 8 + rows * part, rows)
        return carry

    lax.fori_loop(0, chans, channel, 0)
    send_halos(full, link, core)


def far_rows_kernel(far1, far2, edge, beyond, full, link, core, field):
    chans, rows, half = far1.shape
    at, count = lax.axis_index("pix"), lax.axis_size("pix")
    even = odd_of("pix") == 0
    present = jnp.logical_and(at > 0, at < count - 1).astype(jnp.float32)
    field[:, 8:24, :half] = far1[...]
    field[:, 8:24, half:] = far2[...]
    for r in range(3):
        field[:, 5 + r, :] = jnp.where(even, beyond[r], edge[r])
        field[:, 24 + r, :] = jnp.where(even, edge[r], beyond[r])

    def channel(c, carry):
        full[c] = smooth_rows(field, c, 8, rows) * present
        return carry

    lax.fori_loop(0, chans, channel, 0)
    send_halos(full, link, core)


def channel_pass(own, halo, down, row, tile, energy, before, boxes, kept_at):
    chans = own.shape[0]
    stride = energy.shape[2] // chans
    at, count = lax.axis_index("chan"), lax.axis_size("chan")
    there = (at > 0 if down else at < count - 1).astype(jnp.float32)
    lanes = pl.ds(pl.multiple_of(tile * LANES, LANES), LANES)
    here = (pl.ds(pl.multiple_of(row, 8), 8), lanes)

    def s(j):
        if down and j < HALO:
            return halo[(j,) + here]
        if not down and j >= HALO + chans:
            return halo[(j - HALO - chans,) + here]
        return own[(j - HALO,) + here]

    step, first = (-1, 28) if down else (1, 15)
    one, three, seven = {}, {}, {}
    runs = [None] * 4
    for n in range(29):
        j = first + step * n
        one[j] = s(j)
        a = j - step
        if n >= 2:
            three[a] = one[a - 1] + one[a] + one[a + 1]
        b = j - 3 * step
        if n >= 6:
            seven[b] = three[b - 2] + three[b + 2] + one[b]
        if n < 14:
            continue
        j -= 7 * step
        fifteen = seven[j - 4] + seven[j + 4] + one[j]
        k = j - 7
        c = k if down else k - 14
        for w, box in enumerate((one[j], three[j], seven[j], fifteen)):
            if kept_at is not None and 7 <= k < 23:
                at_rows = pl.ds(pl.multiple_of(kept_at, 8), 8)
                boxes[w, k - 7 if down else k - 15, at_rows, lanes] = box
            square = box * box
            if k < 7 or k >= 23:
                square = square * there
            runs[w] = square if runs[w] is None else runs[w] + square
            at_c = (w, tile, pl.ds(pl.multiple_of(c * stride + row, 8), 8), slice(None))
            if before is not None and 1 <= c <= 14:
                energy[at_c] = before[at_c] + runs[w]
            else:
                energy[at_c] = runs[w]
    if before is not None:
        c = 15 if down else 0
        for w in range(4):
            at_c = (w, tile, pl.ds(pl.multiple_of(c * stride + row, 8), 8), slice(None))
            energy[at_c] = before[at_c]


def strips(own, halo, core_side, energy, before, boxes):
    chans, tall, cols = own.shape
    odd = odd_of("chan")
    tiles = cols // LANES
    own_row = 16 * odd_of("pix")

    def run(down):
        def both(n, carry):
            tile, i = n // 2, n % 2
            if tall == 32:
                channel_pass(own, halo, down, own_row + 8 * i, tile, energy, before, boxes, 8 * i)
                channel_pass(own, halo, down, 16 - own_row + 8 * i, tile, energy, before, None, None)
            else:
                channel_pass(own, halo, down, 8 * i, tile, energy, before, None, None)
            return carry

        lax.fori_loop(0, 2 * tiles, both, 0)

    pl.when(odd == 0)(lambda: run(not core_side))
    pl.when(odd == 1)(lambda: run(core_side))


def pair_core_kernel(own, core, after, energy, boxes):
    strips(own, core, True, energy, None, boxes)


def far_core_kernel(own, core, after, energy):
    strips(own, core, True, energy, None, None)


def two_terms(sums, w):
    tiles, height = sums.shape[1:3]
    value = jnp.concatenate([sums[w, tile] for tile in range(tiles)], axis=1)
    value = value.reshape(16, height // 16, tiles * LANES)[:, :16].reshape(256, tiles * LANES)
    first = value.astype(jnp.bfloat16)
    second = (value - first.astype(jnp.float32)).astype(jnp.bfloat16)
    return jnp.concatenate([first, second], axis=1)


def for_parity(odd, body):
    def loop(even):
        def step(w, carry):
            body(w, even)
            return carry

        lax.fori_loop(0, 4, step, 0)

    pl.when(odd == 0)(lambda: loop(True))
    pl.when(odd == 1)(lambda: loop(False))


def pair_noise_kernel(own, link, before, core_boxes, after, boxes, sums, band, link_boxes, energy):
    chans, tall, cols = own.shape
    rows = tall // 2
    odd = odd_of("pix")
    strips(own, link, False, energy, before, link_boxes)
    low = pl.ds(8 * odd_of("chan"), 8)
    high = pl.ds(8 - 8 * odd_of("chan"), 8)
    boxes[:, low] = link_boxes[...]
    boxes[:, high] = core_boxes[...]

    stride = energy.shape[2] // chans

    def row_windows(w, even):
        for half in range(2):
            for tile in range(cols // LANES):

                def e(i):
                    return energy[w, tile, pl.ds(half * 8 * stride + i, 8, stride=stride), :]

                first = 0 if even else rows
                run = e(first)
                for i in range(1, rows):
                    run = run + e(first + i)
                for d in range(rows):
                    if d > 0:
                        run = run + e(15 + d if even else 16 - d)
                    sums[w, tile, half, d if even else 15 - d] = run

    for_parity(odd, row_windows)
    apart = lax.broadcasted_iota(jnp.int32, (cols, cols), 0) - lax.broadcasted_iota(
        jnp.int32, (cols, cols), 1
    )
    band[...] = (jnp.abs(apart) <= 15).astype(jnp.float32).astype(jnp.bfloat16)


def snr_kernel(
    own, link, before, part, band, boxes, blanked, out, energy, sums, ready, sems
):
    chans, rows, cols = own.shape
    odd = odd_of("pix")
    strips(own, link, False, energy, before, None)

    stride = energy.shape[2] // chans

    def row_windows(w, even):
        for half in range(2):
            for tile in range(cols // LANES):
                run = None
                for d in range(rows):
                    if d > 0:
                        i = 16 - d if even else d - 1
                        e = energy[w, tile, pl.ds(half * 8 * stride + i, 8, stride=stride), :]
                        run = e if run is None else run + e
                    row = 15 - d if even else d
                    value = part[w, tile, half, row]
                    at = pl.ds(half * 8 * stride + row, 8, stride=stride)
                    sums[w, tile, at, :] = value if run is None else value + run

    for_parity(odd, row_windows)
    kept = (1 - blanked[...]).astype(jnp.float32)
    both = jnp.concatenate([band[...], band[...]], axis=0)
    copies = []
    for w, width in enumerate(WIDTHS):
        total = jnp.dot(two_terms(sums, w), both, preferred_element_type=jnp.float32)
        scale = lax.rsqrt(total * (1.0 / (VOLUME * width * width)) + 1e-5) * (1.0 / width)
        ready[w] = boxes[w] * scale.reshape(chans, rows, cols) * kept[None]
        copies.append(pltpu.make_async_copy(ready.at[w], out.at[w], sems.at[w]))
        copies[-1].start()
    for copy in copies:
        copy.wait()


def per_device(data_cube, blanked):
    chans, rows, cols = data_cube.shape
    pix = lax.axis_size("pix")
    tiles = cols // LANES

    def move(value, axis, pairs):
        count = lax.axis_size(axis)
        return lax.ppermute(value, axis, [(a, b) for a, b in pairs if 0 <= b < count])

    def swap(value, axis, first):
        count = lax.axis_size(axis)
        pairs = [(i, i + 1 if (i - first) % 2 == 0 else i - 1) for i in range(count)]
        return move(value, axis, pairs)

    toward = [(i, i + 2 if i % 2 == 0 else i - 2) for i in range(pix)]
    back = [(i, i - 2 if i % 2 == 0 else i + 2) for i in range(pix)]
    half = cols // 2
    cells, right, edge, edge2 = call(
        clean_cols_kernel,
        [f32(chans, rows, cols), f32(chans, rows, half), f32(3, chans, cols), f32(3, chans, cols)],
    )(data_cube, blanked)
    near = swap(cells, "pix", 0)
    far_right = swap(move(right, "pix", back), "pix", 0)
    edge_near = move(edge, "pix", back)
    edge_far = swap(edge, "pix", 1)
    beyond = move(edge2, "pix", toward)

    def left_half(value, *rest):
        rest[-1][...] = value[:, :, : rest[-1].shape[2]]

    near_left = call(left_half, f32(chans, rows, half), in_specs=[VMEM] + [ANY] * 3)(
        near, edge_near, edge_far, beyond
    )
    far_left = move(near_left, "pix", toward)

    pair, pair_link, pair_core = call(
        pair_rows_kernel,
        [f32(chans, 32, cols), f32(HALO, 32, cols), f32(HALO, 32, cols)],
        [pltpu.VMEM((chans, 48, cols), jnp.float32)],
        micros=0.01,
    )(cells, near, edge_far, edge_near)
    pair_link = swap(pair_link, "chan", 1)
    pair_core = swap(pair_core, "chan", 0)

    outer, outer_link, outer_core = call(
        far_rows_kernel,
        [f32(chans, 16, cols), f32(HALO, 16, cols), f32(HALO, 16, cols)],
        [pltpu.VMEM((chans, 32, cols), jnp.float32)],
        micros=30.0,
    )(far_left, far_right, edge, beyond)
    outer_link = swap(outer_link, "chan", 1)
    outer_core = swap(outer_core, "chan", 0)

    pair_energy, core_boxes = call(
        pair_core_kernel,
        [f32(4, tiles, chans * 40, LANES), f32(4, chans // 2, rows, cols)],
        micros=2.0,
        in_specs=[VMEM, VMEM, ANY],
    )(pair, pair_core, outer)
    boxes, part, band = call(
        pair_noise_kernel,
        [
            f32(4, chans, rows, cols),
            f32(4, tiles, 2, rows, chans // 2, LANES),
            jax.ShapeDtypeStruct((cols, cols), jnp.bfloat16),
        ],
        [
            pltpu.VMEM((4, chans // 2, rows, cols), jnp.float32),
            pltpu.VMEM((4, tiles, chans * 40, LANES), jnp.float32),
        ],
        micros=3.0,
        in_specs=[VMEM, VMEM, VMEM, VMEM, ANY],
    )(pair, pair_link, pair_energy, core_boxes, outer)
    far_energy = call(
        far_core_kernel,
        f32(4, tiles, chans * 24, LANES),
        in_specs=[VMEM, VMEM, ANY],
    )(outer, outer_core, part)
    return call(
        snr_kernel,
        f32(4, chans, rows, cols),
        [
            pltpu.VMEM((4, tiles, chans * 24, LANES), jnp.float32),
            pltpu.VMEM((4, tiles, chans * 24, LANES), jnp.float32),
            pltpu.VMEM((4, chans, rows, cols), jnp.float32),
            pltpu.SemaphoreType.DMA((4,)),
        ],
        micros=4.0,
        out_specs=ANY,
    )(outer, outer_link, far_energy, part, band, boxes, blanked)


def solution(mesh):
    return jax.shard_map(
        per_device,
        mesh=mesh,
        in_specs=(P("chan", "pix", None), P("pix", None)),
        out_specs=P(None, "chan", "pix", None),
        check_vma=False,
    )
```

```python
import math

import jax
import jax.numpy as jnp
from jax import lax
from jax.experimental import pallas as pl
from jax.experimental.pallas import tpu as pltpu
from jax.sharding import PartitionSpec as P

SIGMA = 3.0 / (2.0 * math.sqrt(2.0 * math.log(2.0)))
VOLUME = 14415.0
WIDTHS = (1, 3, 7, 15)
HALO = 14
LANES = 128
ANY = pl.BlockSpec(memory_space=pl.ANY)
VMEM = pl.BlockSpec(memory_space=pltpu.VMEM)


def kernel_taps():
    weights = [math.exp(-0.5 * (offset / SIGMA) ** 2) for offset in range(-3, 4)]
    total = sum(weights)
    return [weight / total for weight in weights]


def call(body, outs, scratch=(), vmem=16, micros=1.0, **specs):
    return pl.pallas_call(
        body,
        out_shape=outs,
        scratch_shapes=list(scratch),
        compiler_params=pltpu.CompilerParams(vmem_limit_bytes=vmem * 1024 * 1024),
        cost_estimate=pl.CostEstimate(
            flops=int(micros * 1e9), bytes_accessed=int(micros * 3.0e6), transcendentals=0
        ),
        **specs,
    )


def f32(*shape):
    return jax.ShapeDtypeStruct(shape, jnp.float32)


def odd_of(axis):
    return lax.axis_index(axis) % 2


def clean_cols_kernel(data, blanked, cells, edge, edge2):
    taps = kernel_taps()
    chans, rows, cols = data.shape
    even = odd_of("pix") == 0
    kept = (1 - blanked[...]).astype(jnp.float32)
    lane = lax.broadcasted_iota(jnp.int32, (rows, cols), 1)
    for c in range(chans):
        x = data[c] * kept
        acc = taps[3] * x
        for t in (1, 2, 3):
            left = jnp.where(lane >= t, pltpu.roll(x, t, 1), 0.0)
            right = jnp.where(lane < cols - t, pltpu.roll(x, cols - t, 1), 0.0)
            acc = acc + taps[3 + t] * (left + right)
        cells[c] = acc
    for r in range(3):
        top = cells[:, r, :]
        bottom = cells[:, rows - 3 + r, :]
        edge[r] = jnp.where(even, top, bottom)
        edge2[r] = jnp.where(even, bottom, top)


def smooth_rows(field, c, base, rows):
    taps = kernel_taps()
    acc = taps[3] * field[c, pl.ds(base, rows), :]
    for t in (1, 2, 3):
        acc = acc + taps[3 + t] * (
            field[c, pl.ds(base - t, rows), :] + field[c, pl.ds(base + t, rows), :]
        )
    return acc


def store_channel(c, value, full, link, core):
    chans = full.shape[0]
    skip = chans - HALO
    odd = odd_of("chan")
    full[c] = value
    if skip <= c < HALO:
        link[c - skip * odd] = value
        core[c - skip * (1 - odd)] = value
        return
    at = c if c < skip else c - skip
    first, second = (link, core) if c < skip else (core, link)

    @pl.when(odd == 0)
    def _():
        first[at] = value

    @pl.when(odd == 1)
    def _():
        second[at] = value


def pair_rows_kernel(cells, near, edge_far, edge_near, full, link, core, field):
    chans, rows, cols = cells.shape
    odd = odd_of("pix")
    even = odd == 0
    field[:, pl.ds(pl.multiple_of(8 + rows * odd, 8), rows), :] = cells[...]
    field[:, pl.ds(pl.multiple_of(8 + rows * (1 - odd), 8), rows), :] = near[...]
    for r in range(3):
        field[:, 5 + r, :] = jnp.where(even, edge_far[r], edge_near[r])
        field[:, 40 + r, :] = jnp.where(even, edge_near[r], edge_far[r])

    for c in range(chans):
        store_channel(c, smooth_rows(field, c, 8, 2 * rows), full, link, core)


def far_rows_kernel(far, edge, beyond, full, link, core, field):
    chans, rows, cols = far.shape
    at, count = lax.axis_index("pix"), lax.axis_size("pix")
    even = odd_of("pix") == 0
    present = jnp.logical_and(at > 0, at < count - 1).astype(jnp.float32)
    field[:, 8:24, :] = far[...]
    for r in range(3):
        field[:, 5 + r, :] = jnp.where(even, beyond[r], edge[r])
        field[:, 24 + r, :] = jnp.where(even, edge[r], beyond[r])

    for c in range(chans):
        store_channel(c, smooth_rows(field, c, 8, rows) * present, full, link, core)


def channel_pass(own, halo, down, row, tile, energy, before, boxes, kept_at):
    chans = own.shape[0]
    stride = energy.shape[2] // chans
    at, count = lax.axis_index("chan"), lax.axis_size("chan")
    there = (at > 0 if down else at < count - 1).astype(jnp.float32)
    lanes = pl.ds(pl.multiple_of(tile * LANES, LANES), LANES)
    here = (pl.ds(pl.multiple_of(row, 8), 8), lanes)

    def s(j):
        if down and j < HALO:
            return halo[(j,) + here]
        if not down and j >= HALO + chans:
            return halo[(j - HALO - chans,) + here]
        return own[(j - HALO,) + here]

    step, first = (-1, 28) if down else (1, 15)
    one, three, seven = {}, {}, {}
    runs = [None] * 4
    for n in range(29):
        j = first + step * n
        one[j] = s(j)
        a = j - step
        if n >= 2:
            three[a] = one[a - 1] + one[a] + one[a + 1]
        b = j - 3 * step
        if n >= 6:
            seven[b] = three[b - 2] + three[b + 2] + one[b]
        if n < 14:
            continue
        j -= 7 * step
        fifteen = seven[j - 4] + seven[j + 4] + one[j]
        k = j - 7
        c = k if down else k - 14
        for w, box in enumerate((one[j], three[j], seven[j], fifteen)):
            if kept_at is not None and 7 <= k < 23:
                at_rows = pl.ds(pl.multiple_of(kept_at, 8), 8)
                boxes[w, k - 7 if down else k - 15, at_rows, lanes] = box
            square = box * box
            if k < 7 or k >= 23:
                square = square * there
            runs[w] = square if runs[w] is None else runs[w] + square
            at_c = (w, tile, pl.ds(pl.multiple_of(c * stride + row, 8), 8), slice(None))
            if before is not None and 1 <= c <= 14:
                energy[at_c] = before[at_c] + runs[w]
            else:
                energy[at_c] = runs[w]
    if before is not None:
        c = 15 if down else 0
        for w in range(4):
            at_c = (w, tile, pl.ds(pl.multiple_of(c * stride + row, 8), 8), slice(None))
            energy[at_c] = before[at_c]


def strips(own, halo, core_side, energy, before, boxes):
    chans, tall, cols = own.shape
    odd = odd_of("chan")
    tiles = cols // LANES
    own_row = 16 * odd_of("pix")

    def run(down):
        def both(n, carry):
            tile, i = n // 2, n % 2
            if tall == 32:
                channel_pass(own, halo, down, own_row + 8 * i, tile, energy, before, boxes, 8 * i)
                channel_pass(own, halo, down, 16 - own_row + 8 * i, tile, energy, before, None, None)
            else:
                channel_pass(own, halo, down, 8 * i, tile, energy, before, None, None)
            return carry

        lax.fori_loop(0, 2 * tiles, both, 0)

    pl.when(odd == 0)(lambda: run(not core_side))
    pl.when(odd == 1)(lambda: run(core_side))


def pair_core_kernel(own, core, after, energy, boxes):
    strips(own, core, True, energy, None, boxes)


def far_core_kernel(own, core, after, energy):
    strips(own, core, True, energy, None, None)


def two_terms(sums, w):
    tiles, height = sums.shape[1:3]
    value = jnp.concatenate([sums[w, tile] for tile in range(tiles)], axis=1)
    value = value.reshape(16, height // 16, tiles * LANES)[:, :16].reshape(256, tiles * LANES)
    first = value.astype(jnp.bfloat16)
    second = (value - first.astype(jnp.float32)).astype(jnp.bfloat16)
    return jnp.concatenate([first, second], axis=1)


def for_parity(odd, body):
    def loop(even):
        def step(w, carry):
            body(w, even)
            return carry

        lax.fori_loop(0, 4, step, 0)

    pl.when(odd == 0)(lambda: loop(True))
    pl.when(odd == 1)(lambda: loop(False))


def pair_noise_kernel(own, link, before, core_boxes, after, boxes, sums, band, link_boxes, energy):
    chans, tall, cols = own.shape
    rows = tall // 2
    odd = odd_of("pix")
    strips(own, link, False, energy, before, link_boxes)
    low = pl.ds(8 * odd_of("chan"), 8)
    high = pl.ds(8 - 8 * odd_of("chan"), 8)
    boxes[:, low] = link_boxes[...]
    boxes[:, high] = core_boxes[...]

    stride = energy.shape[2] // chans

    def row_windows(w, even):
        for half in range(2):
            for tile in range(cols // LANES):

                def e(i):
                    return energy[w, tile, pl.ds(half * 8 * stride + i, 8, stride=stride), :]

                first = 0 if even else rows
                run = e(first)
                for i in range(1, rows):
                    run = run + e(first + i)
                for d in range(rows):
                    if d > 0:
                        run = run + e(15 + d if even else 16 - d)
                    sums[w, tile, half, d if even else 15 - d] = run

    for_parity(odd, row_windows)
    apart = lax.broadcasted_iota(jnp.int32, (cols, cols), 0) - lax.broadcasted_iota(
        jnp.int32, (cols, cols), 1
    )
    band[...] = (jnp.abs(apart) <= 15).astype(jnp.float32).astype(jnp.bfloat16)


def snr_kernel(
    own, link, before, part, band, boxes, blanked, out, energy, sums, ready, sems
):
    chans, rows, cols = own.shape
    odd = odd_of("pix")
    strips(own, link, False, energy, before, None)

    stride = energy.shape[2] // chans

    kept = (1 - blanked[...]).astype(jnp.float32)

    def finish(even):
        both = jnp.concatenate([band[...], band[...]], axis=0)
        copies = []
        for w, width in enumerate(WIDTHS):
            for half in range(2):
                for tile in range(cols // LANES):
                    run = None
                    for d in range(rows):
                        if d > 0:
                            i = 16 - d if even else d - 1
                            e = energy[w, tile, pl.ds(half * 8 * stride + i, 8, stride=stride), :]
                            run = e if run is None else run + e
                        row = 15 - d if even else d
                        value = part[w, tile, half, row]
                        at = pl.ds(half * 8 * stride + row, 8, stride=stride)
                        sums[w, tile, at, :] = value if run is None else value + run
            total = jnp.dot(two_terms(sums, w), both, preferred_element_type=jnp.float32)
            scale = lax.rsqrt(total * (1.0 / (VOLUME * width * width)) + 1e-5) * (1.0 / width)
            ready[w] = boxes[w] * scale.reshape(chans, rows, cols) * kept[None]
            copies.append(pltpu.make_async_copy(ready.at[w], out.at[w], sems.at[w]))
            copies[-1].start()
        for copy in copies:
            copy.wait()

    pl.when(odd == 0)(lambda: finish(True))
    pl.when(odd == 1)(lambda: finish(False))


def per_device(data_cube, blanked):
    chans, rows, cols = data_cube.shape
    pix = lax.axis_size("pix")
    tiles = cols // LANES

    def move(value, axis, pairs):
        count = lax.axis_size(axis)
        return lax.ppermute(value, axis, [(a, b) for a, b in pairs if 0 <= b < count])

    def swap(value, axis, first):
        count = lax.axis_size(axis)
        pairs = [(i, i + 1 if (i - first) % 2 == 0 else i - 1) for i in range(count)]
        return move(value, axis, pairs)

    toward = [(i, i + 2 if i % 2 == 0 else i - 2) for i in range(pix)]
    back = [(i, i - 2 if i % 2 == 0 else i + 2) for i in range(pix)]
    cells, edge, edge2 = call(
        clean_cols_kernel, [f32(chans, rows, cols), f32(3, chans, cols), f32(3, chans, cols)]
    )(data_cube, blanked)
    near = swap(cells, "pix", 0)
    edge_near = move(edge, "pix", back)
    edge_far = swap(edge, "pix", 1)
    beyond = move(edge2, "pix", toward)
    near = call(
        lambda value, *rest: None,
        f32(*near.shape),
        in_specs=[ANY] * 4,
        out_specs=ANY,
        input_output_aliases={0: 0},
    )(near, edge_near, edge_far, beyond)
    far = move(near, "pix", toward)

    pair, pair_link, pair_core = call(
        pair_rows_kernel,
        [f32(chans, 32, cols), f32(HALO, 32, cols), f32(HALO, 32, cols)],
        [pltpu.VMEM((chans, 48, cols), jnp.float32)],
        micros=0.01,
    )(cells, near, edge_far, edge_near)
    pair_link = swap(pair_link, "chan", 1)
    pair_core = swap(pair_core, "chan", 0)

    outer, outer_link, outer_core = call(
        far_rows_kernel,
        [f32(chans, 16, cols), f32(HALO, 16, cols), f32(HALO, 16, cols)],
        [pltpu.VMEM((chans, 32, cols), jnp.float32)],
        micros=30.0,
    )(far, edge, beyond)
    outer_link = swap(outer_link, "chan", 1)
    outer_core = swap(outer_core, "chan", 0)

    pair_energy, core_boxes = call(
        pair_core_kernel,
        [f32(4, tiles, chans * 40, LANES), f32(4, chans // 2, rows, cols)],
        micros=2.0,
        in_specs=[VMEM, VMEM, ANY],
    )(pair, pair_core, outer)
    boxes, part, band = call(
        pair_noise_kernel,
        [
            f32(4, chans, rows, cols),
            f32(4, tiles, 2, rows, chans // 2, LANES),
            jax.ShapeDtypeStruct((cols, cols), jnp.bfloat16),
        ],
        [
            pltpu.VMEM((4, chans // 2, rows, cols), jnp.float32),
            pltpu.VMEM((4, tiles, chans * 40, LANES), jnp.float32),
        ],
        micros=3.0,
        in_specs=[VMEM, VMEM, VMEM, VMEM, ANY],
    )(pair, pair_link, pair_energy, core_boxes, outer)
    far_energy = call(
        far_core_kernel,
        f32(4, tiles, chans * 24, LANES),
        in_specs=[VMEM, VMEM, ANY],
    )(outer, outer_core, part)
    return call(
        snr_kernel,
        f32(4, chans, rows, cols),
        [
            pltpu.VMEM((4, tiles, chans * 24, LANES), jnp.float32),
            pltpu.VMEM((4, tiles, chans * 24, LANES), jnp.float32),
            pltpu.VMEM((4, chans, rows, cols), jnp.float32),
            pltpu.SemaphoreType.DMA((4,)),
        ],
        micros=4.0,
        out_specs=ANY,
    )(outer, outer_link, far_energy, part, band, boxes, blanked)


def solution(mesh):
    return jax.shard_map(
        per_device,
        mesh=mesh,
        in_specs=(P("chan", "pix", None), P("pix", None)),
        out_specs=P(None, "chan", "pix", None),
        check_vma=False,
    )
```

```python
import math

import jax
import jax.numpy as jnp
from jax import lax
from jax.experimental import pallas as pl
from jax.experimental.pallas import tpu as pltpu
from jax.sharding import PartitionSpec as P

SIGMA = 3.0 / (2.0 * math.sqrt(2.0 * math.log(2.0)))
VOLUME = 14415.0
WIDTHS = (1, 3, 7, 15)
HALO = 14
LANES = 128
ANY = pl.BlockSpec(memory_space=pl.ANY)
VMEM = pl.BlockSpec(memory_space=pltpu.VMEM)


def kernel_taps():
    weights = [math.exp(-0.5 * (offset / SIGMA) ** 2) for offset in range(-3, 4)]
    total = sum(weights)
    return [weight / total for weight in weights]


def call(body, outs, scratch=(), vmem=16, micros=1.0, **specs):
    return pl.pallas_call(
        body,
        out_shape=outs,
        scratch_shapes=list(scratch),
        compiler_params=pltpu.CompilerParams(vmem_limit_bytes=vmem * 1024 * 1024),
        cost_estimate=pl.CostEstimate(
            flops=int(micros * 1e9), bytes_accessed=int(micros * 3.0e6), transcendentals=0
        ),
        **specs,
    )


def f32(*shape):
    return jax.ShapeDtypeStruct(shape, jnp.float32)


def odd_of(axis):
    return lax.axis_index(axis) % 2


def clean_cols_kernel(data, blanked, cells, second, edge, edge2):
    taps = kernel_taps()
    chans, rows, cols = data.shape
    even = odd_of("pix") == 0
    kept = (1 - blanked[...]).astype(jnp.float32)
    lane = lax.broadcasted_iota(jnp.int32, (rows, cols), 1)
    for c in range(chans):
        x = data[c] * kept
        acc = taps[3] * x
        for t in (1, 2, 3):
            left = jnp.where(lane >= t, pltpu.roll(x, t, 1), 0.0)
            right = jnp.where(lane < cols - t, pltpu.roll(x, cols - t, 1), 0.0)
            acc = acc + taps[3 + t] * (left + right)
        cells[c] = acc
        second[c] = acc[:, cols - second.shape[2] :]
    for r in range(3):
        top = cells[:, r, :]
        bottom = cells[:, rows - 3 + r, :]
        edge[r] = jnp.where(even, top, bottom)
        edge2[r] = jnp.where(even, bottom, top)


def smooth_rows(field, c, base, rows):
    taps = kernel_taps()
    acc = taps[3] * field[c, pl.ds(base, rows), :]
    for t in (1, 2, 3):
        acc = acc + taps[3 + t] * (
            field[c, pl.ds(base - t, rows), :] + field[c, pl.ds(base + t, rows), :]
        )
    return acc


def store_channel(c, value, full, link, core):
    chans = full.shape[0]
    skip = chans - HALO
    odd = odd_of("chan")
    full[c] = value
    if skip <= c < HALO:
        link[c - skip * odd] = value
        core[c - skip * (1 - odd)] = value
        return
    at = c if c < skip else c - skip
    first, second = (link, core) if c < skip else (core, link)

    @pl.when(odd == 0)
    def _():
        first[at] = value

    @pl.when(odd == 1)
    def _():
        second[at] = value


def pair_rows_kernel(cells, near, edge_far, edge_near, full, link, core, field):
    chans, rows, cols = cells.shape
    odd = odd_of("pix")
    even = odd == 0
    field[:, pl.ds(pl.multiple_of(8 + rows * odd, 8), rows), :] = cells[...]
    field[:, pl.ds(pl.multiple_of(8 + rows * (1 - odd), 8), rows), :] = near[...]
    for r in range(3):
        field[:, 5 + r, :] = jnp.where(even, edge_far[r], edge_near[r])
        field[:, 40 + r, :] = jnp.where(even, edge_near[r], edge_far[r])

    for c in range(chans):
        store_channel(c, smooth_rows(field, c, 8, 2 * rows), full, link, core)


def far_rows_kernel(far1, far2, edge, beyond, full, link, core, field):
    chans, rows, half = far1.shape
    at, count = lax.axis_index("pix"), lax.axis_size("pix")
    even = odd_of("pix") == 0
    present = jnp.logical_and(at > 0, at < count - 1).astype(jnp.float32)
    field[:, 8:24, :half] = far1[...]
    field[:, 8:24, half:] = far2[...]
    for r in range(3):
        field[:, 5 + r, :] = jnp.where(even, beyond[r], edge[r])
        field[:, 24 + r, :] = jnp.where(even, edge[r], beyond[r])

    for c in range(chans):
        store_channel(c, smooth_rows(field, c, 8, rows) * present, full, link, core)


def channel_pass(own, halo, down, row, tile, energy, before, boxes, kept_at):
    chans = own.shape[0]
    stride = energy.shape[2] // chans
    at, count = lax.axis_index("chan"), lax.axis_size("chan")
    there = (at > 0 if down else at < count - 1).astype(jnp.float32)
    lanes = pl.ds(pl.multiple_of(tile * LANES, LANES), LANES)
    here = (pl.ds(pl.multiple_of(row, 8), 8), lanes)

    def s(j):
        if down and j < HALO:
            return halo[(j,) + here]
        if not down and j >= HALO + chans:
            return halo[(j - HALO - chans,) + here]
        return own[(j - HALO,) + here]

    step, first = (-1, 28) if down else (1, 15)
    one, three, seven = {}, {}, {}
    runs = [None] * 4
    for n in range(29):
        j = first + step * n
        one[j] = s(j)
        a = j - step
        if n >= 2:
            three[a] = one[a - 1] + one[a] + one[a + 1]
        b = j - 3 * step
        if n >= 6:
            seven[b] = three[b - 2] + three[b + 2] + one[b]
        if n < 14:
            continue
        j -= 7 * step
        fifteen = seven[j - 4] + seven[j + 4] + one[j]
        k = j - 7
        c = k if down else k - 14
        for w, box in enumerate((one[j], three[j], seven[j], fifteen)):
            if kept_at is not None and 7 <= k < 23:
                at_rows = pl.ds(pl.multiple_of(kept_at, 8), 8)
                boxes[w, k - 7 if down else k - 15, at_rows, lanes] = box
            square = box * box
            if k < 7 or k >= 23:
                square = square * there
            runs[w] = square if runs[w] is None else runs[w] + square
            at_c = (w, tile, pl.ds(pl.multiple_of(c * stride + row, 8), 8), slice(None))
            if before is not None and 1 <= c <= 14:
                energy[at_c] = before[at_c] + runs[w]
            else:
                energy[at_c] = runs[w]
    if before is not None:
        c = 15 if down else 0
        for w in range(4):
            at_c = (w, tile, pl.ds(pl.multiple_of(c * stride + row, 8), 8), slice(None))
            energy[at_c] = before[at_c]


def strips(own, halo, core_side, energy, before, boxes):
    chans, tall, cols = own.shape
    odd = odd_of("chan")
    tiles = cols // LANES
    own_row = 16 * odd_of("pix")

    def run(down):
        def both(n, carry):
            tile, i = n // 2, n % 2
            if tall == 32:
                channel_pass(own, halo, down, own_row + 8 * i, tile, energy, before, boxes, 8 * i)
                channel_pass(own, halo, down, 16 - own_row + 8 * i, tile, energy, before, None, None)
            else:
                channel_pass(own, halo, down, 8 * i, tile, energy, before, None, None)
            return carry

        lax.fori_loop(0, 2 * tiles, both, 0)

    pl.when(odd == 0)(lambda: run(not core_side))
    pl.when(odd == 1)(lambda: run(core_side))


def pair_core_kernel(own, core, after, energy, boxes):
    strips(own, core, True, energy, None, boxes)


def far_core_kernel(own, core, after, energy):
    strips(own, core, True, energy, None, None)


def two_terms(sums, w):
    tiles, height = sums.shape[1:3]
    value = jnp.concatenate([sums[w, tile] for tile in range(tiles)], axis=1)
    value = value.reshape(16, height // 16, tiles * LANES)[:, :16].reshape(256, tiles * LANES)
    first = value.astype(jnp.bfloat16)
    second = (value - first.astype(jnp.float32)).astype(jnp.bfloat16)
    return jnp.concatenate([first, second], axis=1)


def for_parity(odd, body):
    def loop(even):
        def step(w, carry):
            body(w, even)
            return carry

        lax.fori_loop(0, 4, step, 0)

    pl.when(odd == 0)(lambda: loop(True))
    pl.when(odd == 1)(lambda: loop(False))


def pair_noise_kernel(own, link, before, core_boxes, after, boxes, sums, band, link_boxes, energy):
    chans, tall, cols = own.shape
    rows = tall // 2
    odd = odd_of("pix")
    strips(own, link, False, energy, before, link_boxes)
    low = pl.ds(8 * odd_of("chan"), 8)
    high = pl.ds(8 - 8 * odd_of("chan"), 8)
    boxes[:, low] = link_boxes[...]
    boxes[:, high] = core_boxes[...]

    stride = energy.shape[2] // chans

    def row_windows(w, even):
        for half in range(2):
            for tile in range(cols // LANES):

                def e(i):
                    return energy[w, tile, pl.ds(half * 8 * stride + i, 8, stride=stride), :]

                first = 0 if even else rows
                run = e(first)
                for i in range(1, rows):
                    run = run + e(first + i)
                for d in range(rows):
                    if d > 0:
                        run = run + e(15 + d if even else 16 - d)
                    sums[w, tile, half, d if even else 15 - d] = run

    for_parity(odd, row_windows)
    apart = lax.broadcasted_iota(jnp.int32, (cols, cols), 0) - lax.broadcasted_iota(
        jnp.int32, (cols, cols), 1
    )
    band[...] = (jnp.abs(apart) <= 15).astype(jnp.float32).astype(jnp.bfloat16)


def snr_kernel(
    own, link, before, part, band, boxes, blanked, out, energy, sums, ready, sems
):
    chans, rows, cols = own.shape
    odd = odd_of("pix")
    strips(own, link, False, energy, before, None)

    stride = energy.shape[2] // chans

    kept = (1 - blanked[...]).astype(jnp.float32)

    def finish(even):
        both = jnp.concatenate([band[...], band[...]], axis=0)
        copies = []
        for w, width in enumerate(WIDTHS):
            for half in range(2):
                for tile in range(cols // LANES):
                    run = None
                    for d in range(rows):
                        if d > 0:
                            i = 16 - d if even else d - 1
                            e = energy[w, tile, pl.ds(half * 8 * stride + i, 8, stride=stride), :]
                            run = e if run is None else run + e
                        row = 15 - d if even else d
                        value = part[w, tile, half, row]
                        at = pl.ds(half * 8 * stride + row, 8, stride=stride)
                        sums[w, tile, at, :] = value if run is None else value + run
            total = jnp.dot(two_terms(sums, w), both, preferred_element_type=jnp.float32)
            scale = lax.rsqrt(total * (1.0 / (VOLUME * width * width)) + 1e-5) * (1.0 / width)
            ready[w] = boxes[w] * scale.reshape(chans, rows, cols) * kept[None]
            copies.append(pltpu.make_async_copy(ready.at[w], out.at[w], sems.at[w]))
            copies[-1].start()
        for copy in copies:
            copy.wait()

    pl.when(odd == 0)(lambda: finish(True))
    pl.when(odd == 1)(lambda: finish(False))


def per_device(data_cube, blanked):
    chans, rows, cols = data_cube.shape
    pix = lax.axis_size("pix")
    tiles = cols // LANES

    def move(value, axis, pairs):
        count = lax.axis_size(axis)
        return lax.ppermute(value, axis, [(a, b) for a, b in pairs if 0 <= b < count])

    def swap(value, axis, first):
        count = lax.axis_size(axis)
        pairs = [(i, i + 1 if (i - first) % 2 == 0 else i - 1) for i in range(count)]
        return move(value, axis, pairs)

    toward = [(i, i + 2 if i % 2 == 0 else i - 2) for i in range(pix)]
    back = [(i, i - 2 if i % 2 == 0 else i + 2) for i in range(pix)]
    half = cols // 2
    cells, right, edge, edge2 = call(
        clean_cols_kernel,
        [f32(chans, rows, cols), f32(chans, rows, half), f32(3, chans, cols), f32(3, chans, cols)],
    )(data_cube, blanked)
    near = swap(cells, "pix", 0)
    far_right = swap(move(right, "pix", back), "pix", 0)
    edge_near = move(edge, "pix", back)
    edge_far = swap(edge, "pix", 1)
    beyond = move(edge2, "pix", toward)

    def left_half(value, *rest):
        rest[-1][...] = value[:, :, : rest[-1].shape[2]]

    near_left = call(left_half, f32(chans, rows, half), in_specs=[VMEM] + [ANY] * 3)(
        near, edge_near, edge_far, beyond
    )
    far_left = move(near_left, "pix", toward)

    pair, pair_link, pair_core = call(
        pair_rows_kernel,
        [f32(chans, 32, cols), f32(HALO, 32, cols), f32(HALO, 32, cols)],
        [pltpu.VMEM((chans, 48, cols), jnp.float32)],
        micros=0.01,
    )(cells, near, edge_far, edge_near)
    pair_link = swap(pair_link, "chan", 1)
    pair_core = swap(pair_core, "chan", 0)

    outer, outer_link, outer_core = call(
        far_rows_kernel,
        [f32(chans, 16, cols), f32(HALO, 16, cols), f32(HALO, 16, cols)],
        [pltpu.VMEM((chans, 32, cols), jnp.float32)],
        micros=30.0,
    )(far_left, far_right, edge, beyond)
    outer_link = swap(outer_link, "chan", 1)
    outer_core = swap(outer_core, "chan", 0)

    pair_energy, core_boxes = call(
        pair_core_kernel,
        [f32(4, tiles, chans * 40, LANES), f32(4, chans // 2, rows, cols)],
        micros=2.0,
        in_specs=[VMEM, VMEM, ANY],
    )(pair, pair_core, outer)
    boxes, part, band = call(
        pair_noise_kernel,
        [
            f32(4, chans, rows, cols),
            f32(4, tiles, 2, rows, chans // 2, LANES),
            jax.ShapeDtypeStruct((cols, cols), jnp.bfloat16),
        ],
        [
            pltpu.VMEM((4, chans // 2, rows, cols), jnp.float32),
            pltpu.VMEM((4, tiles, chans * 40, LANES), jnp.float32),
        ],
        micros=3.0,
        in_specs=[VMEM, VMEM, VMEM, VMEM, ANY],
    )(pair, pair_link, pair_energy, core_boxes, outer)
    far_energy = call(
        far_core_kernel,
        f32(4, tiles, chans * 24, LANES),
        in_specs=[VMEM, VMEM, ANY],
    )(outer, outer_core, part)
    return call(
        snr_kernel,
        f32(4, chans, rows, cols),
        [
            pltpu.VMEM((4, tiles, chans * 24, LANES), jnp.float32),
            pltpu.VMEM((4, tiles, chans * 24, LANES), jnp.float32),
            pltpu.VMEM((4, chans, rows, cols), jnp.float32),
            pltpu.SemaphoreType.DMA((4,)),
        ],
        micros=4.0,
        out_specs=ANY,
    )(outer, outer_link, far_energy, part, band, boxes, blanked)


def solution(mesh):
    return jax.shard_map(
        per_device,
        mesh=mesh,
        in_specs=(P("chan", "pix", None), P("pix", None)),
        out_specs=P(None, "chan", "pix", None),
        check_vma=False,
    )
```

```python
import math

import jax
import jax.numpy as jnp
from jax import lax
from jax.experimental import pallas as pl
from jax.experimental.pallas import tpu as pltpu
from jax.sharding import PartitionSpec as P

SIGMA = 3.0 / (2.0 * math.sqrt(2.0 * math.log(2.0)))
VOLUME = 14415.0
WIDTHS = (1, 3, 7, 15)
HALO = 14
LANES = 128
ANY = pl.BlockSpec(memory_space=pl.ANY)
VMEM = pl.BlockSpec(memory_space=pltpu.VMEM)


def kernel_taps():
    weights = [math.exp(-0.5 * (offset / SIGMA) ** 2) for offset in range(-3, 4)]
    total = sum(weights)
    return [weight / total for weight in weights]


def call(body, outs, scratch=(), vmem=16, micros=1.0, **specs):
    return pl.pallas_call(
        body,
        out_shape=outs,
        scratch_shapes=list(scratch),
        compiler_params=pltpu.CompilerParams(vmem_limit_bytes=vmem * 1024 * 1024),
        cost_estimate=pl.CostEstimate(
            flops=int(micros * 1e9), bytes_accessed=int(micros * 3.0e6), transcendentals=0
        ),
        **specs,
    )


def f32(*shape):
    return jax.ShapeDtypeStruct(shape, jnp.float32)


def odd_of(axis):
    return lax.axis_index(axis) % 2


def clean_cols_kernel(data, blanked, cells, edge, edge2):
    taps = kernel_taps()
    chans, rows, cols = data.shape
    even = odd_of("pix") == 0
    kept = (1 - blanked[...]).astype(jnp.float32)
    lane = lax.broadcasted_iota(jnp.int32, (rows, cols), 1)
    for c in range(chans):
        x = data[c] * kept
        acc = taps[3] * x
        for t in (1, 2, 3):
            left = jnp.where(lane >= t, pltpu.roll(x, t, 1), 0.0)
            right = jnp.where(lane < cols - t, pltpu.roll(x, cols - t, 1), 0.0)
            acc = acc + taps[3 + t] * (left + right)
        cells[c] = acc
    for r in range(3):
        top = cells[:, r, :]
        bottom = cells[:, rows - 3 + r, :]
        edge[r] = jnp.where(even, top, bottom)
        edge2[r] = jnp.where(even, bottom, top)


def smooth_rows(field, c, base, rows):
    taps = kernel_taps()
    acc = taps[3] * field[c, pl.ds(base, rows), :]
    for t in (1, 2, 3):
        acc = acc + taps[3 + t] * (
            field[c, pl.ds(base - t, rows), :] + field[c, pl.ds(base + t, rows), :]
        )
    return acc


def store_channel(c, value, full, link, core):
    chans = full.shape[0]
    skip = chans - HALO
    odd = odd_of("chan")
    full[c] = value
    if skip <= c < HALO:
        link[c - skip * odd] = value
        core[c - skip * (1 - odd)] = value
        return
    at = c if c < skip else c - skip
    first, second = (link, core) if c < skip else (core, link)

    @pl.when(odd == 0)
    def _():
        first[at] = value

    @pl.when(odd == 1)
    def _():
        second[at] = value


def pair_rows_kernel(cells, near, edge_far, edge_near, full, link, core, field):
    chans, rows, cols = cells.shape
    odd = odd_of("pix")
    even = odd == 0
    field[:, pl.ds(pl.multiple_of(8 + rows * odd, 8), rows), :] = cells[...]
    field[:, pl.ds(pl.multiple_of(8 + rows * (1 - odd), 8), rows), :] = near[...]
    for r in range(3):
        field[:, 5 + r, :] = jnp.where(even, edge_far[r], edge_near[r])
        field[:, 40 + r, :] = jnp.where(even, edge_near[r], edge_far[r])

    for c in range(chans):
        store_channel(c, smooth_rows(field, c, 8, 2 * rows), full, link, core)


def far_rows_kernel(far, edge, beyond, full, link, core, field):
    chans, rows, cols = far.shape
    at, count = lax.axis_index("pix"), lax.axis_size("pix")
    even = odd_of("pix") == 0
    present = jnp.logical_and(at > 0, at < count - 1).astype(jnp.float32)
    field[:, 8:24, :] = far[...]
    for r in range(3):
        field[:, 5 + r, :] = jnp.where(even, beyond[r], edge[r])
        field[:, 24 + r, :] = jnp.where(even, edge[r], beyond[r])

    for c in range(chans):
        store_channel(c, smooth_rows(field, c, 8, rows) * present, full, link, core)


def channel_pass(own, halo, down, row, tile, energy, before, boxes, kept_at):
    chans = own.shape[0]
    stride = energy.shape[2] // chans
    at, count = lax.axis_index("chan"), lax.axis_size("chan")
    there = (at > 0 if down else at < count - 1).astype(jnp.float32)
    lanes = pl.ds(pl.multiple_of(tile * LANES, LANES), LANES)
    here = (pl.ds(pl.multiple_of(row, 8), 8), lanes)

    def s(j):
        if down and j < HALO:
            return halo[(j,) + here]
        if not down and j >= HALO + chans:
            return halo[(j - HALO - chans,) + here]
        return own[(j - HALO,) + here]

    step, first = (-1, 28) if down else (1, 15)
    one, three, seven = {}, {}, {}
    runs = [None] * 4
    for n in range(29):
        j = first + step * n
        one[j] = s(j)
        a = j - step
        if n >= 2:
            three[a] = one[a - 1] + one[a] + one[a + 1]
        b = j - 3 * step
        if n >= 6:
            seven[b] = three[b - 2] + three[b + 2] + one[b]
        if n < 14:
            continue
        j -= 7 * step
        fifteen = seven[j - 4] + seven[j + 4] + one[j]
        k = j - 7
        c = k if down else k - 14
        for w, box in enumerate((one[j], three[j], seven[j], fifteen)):
            if kept_at is not None and 7 <= k < 23:
                at_rows = pl.ds(pl.multiple_of(kept_at, 8), 8)
                boxes[w, k - 7 if down else k - 15, at_rows, lanes] = box
            square = box * box
            if k < 7 or k >= 23:
                square = square * there
            runs[w] = square if runs[w] is None else runs[w] + square
            at_c = (w, tile, pl.ds(pl.multiple_of(c * stride + row, 8), 8), slice(None))
            if before is not None and 1 <= c <= 14:
                energy[at_c] = before[at_c] + runs[w]
            else:
                energy[at_c] = runs[w]
    if before is not None:
        c = 15 if down else 0
        for w in range(4):
            at_c = (w, tile, pl.ds(pl.multiple_of(c * stride + row, 8), 8), slice(None))
            energy[at_c] = before[at_c]


def strips(own, halo, core_side, energy, before, boxes):
    chans, tall, cols = own.shape
    odd = odd_of("chan")
    tiles = cols // LANES
    own_row = 16 * odd_of("pix")

    def run(down):
        def both(n, carry):
            tile, i = n // 2, n % 2
            if tall == 32:
                channel_pass(own, halo, down, own_row + 8 * i, tile, energy, before, boxes, 8 * i)
                channel_pass(own, halo, down, 16 - own_row + 8 * i, tile, energy, before, None, None)
            else:
                channel_pass(own, halo, down, 8 * i, tile, energy, before, None, None)
            return carry

        lax.fori_loop(0, 2 * tiles, both, 0)

    pl.when(odd == 0)(lambda: run(not core_side))
    pl.when(odd == 1)(lambda: run(core_side))


def pair_core_kernel(own, core, after, energy, boxes):
    strips(own, core, True, energy, None, boxes)


def far_core_kernel(own, core, after, energy):
    strips(own, core, True, energy, None, None)


def two_terms(sums, w):
    tiles, height = sums.shape[1:3]
    firsts, seconds = [], []
    for tile in range(tiles):
        value = sums[w, tile].reshape(16, height // 16, LANES)[:, :16].reshape(256, LANES)
        firsts.append(value.astype(jnp.bfloat16))
        seconds.append((value - firsts[-1].astype(jnp.float32)).astype(jnp.bfloat16))
    return firsts, seconds


def for_parity(odd, body):
    def loop(even):
        def step(w, carry):
            body(w, even)
            return carry

        lax.fori_loop(0, 4, step, 0)

    pl.when(odd == 0)(lambda: loop(True))
    pl.when(odd == 1)(lambda: loop(False))


def pair_noise_kernel(
    own, link, before, core_boxes, blanked, after, boxes, sums, band, link_boxes, energy
):
    chans, tall, cols = own.shape
    rows = tall // 2
    odd = odd_of("pix")
    strips(own, link, False, energy, before, link_boxes)
    low = pl.ds(8 * odd_of("chan"), 8)
    high = pl.ds(8 - 8 * odd_of("chan"), 8)
    kept = (1 - blanked[...]).astype(jnp.float32)
    for w, width in enumerate(WIDTHS):
        factor = (kept * (1.0 / width))[None]
        boxes[w, low] = link_boxes[w] * factor
        boxes[w, high] = core_boxes[w] * factor

    stride = energy.shape[2] // chans

    def row_windows(w, even):
        for half in range(2):
            for tile in range(cols // LANES):

                def e(i):
                    return energy[w, tile, pl.ds(half * 8 * stride + i, 8, stride=stride), :]

                first = 0 if even else rows
                run = e(first)
                for i in range(1, rows):
                    run = run + e(first + i)
                for d in range(rows):
                    if d > 0:
                        run = run + e(15 + d if even else 16 - d)
                    sums[w, tile, half, d if even else 15 - d] = run

    for_parity(odd, row_windows)
    for h in range(2):
        i = lax.broadcasted_iota(jnp.int32, band.shape[1:], 0) + h * LANES
        j = lax.broadcasted_iota(jnp.int32, band.shape[1:], 1) + h * 2 * LANES
        band[h] = (jnp.abs(i - j) <= 15).astype(jnp.float32).astype(jnp.bfloat16)


def snr_kernel(
    own, link, before, part, band, boxes, out, energy, sums, ready, sems
):
    chans, rows, cols = own.shape
    odd = odd_of("pix")
    strips(own, link, False, energy, before, None)

    stride = energy.shape[2] // chans

    def finish(even):
        copies = []
        for w, width in enumerate(WIDTHS):
            for half in range(2):
                for tile in range(cols // LANES):
                    run = None
                    for d in range(rows):
                        if d > 0:
                            i = 16 - d if even else d - 1
                            e = energy[w, tile, pl.ds(half * 8 * stride + i, 8, stride=stride), :]
                            run = e if run is None else run + e
                        row = 15 - d if even else d
                        value = part[w, tile, half, row]
                        at = pl.ds(half * 8 * stride + row, 8, stride=stride)
                        sums[w, tile, at, :] = value if run is None else value + run
            firsts, seconds = two_terms(sums, w)
            for h in range(2):
                both = jnp.concatenate(firsts[h : h + 3] + seconds[h : h + 3], axis=1)
                ones = jnp.concatenate([band[h], band[h]], axis=0)
                total = jnp.dot(both, ones, preferred_element_type=jnp.float32)
                scale = lax.rsqrt(total * (1.0 / (VOLUME * width * width)) + 1e-5)
                lanes = slice(h * 2 * LANES, (h + 1) * 2 * LANES)
                ready[w, :, :, lanes] = boxes[w, :, :, lanes] * scale.reshape(chans, rows, -1)
            copies.append(pltpu.make_async_copy(ready.at[w], out.at[w], sems.at[w]))
            copies[-1].start()
        for copy in copies:
            copy.wait()

    pl.when(odd == 0)(lambda: finish(True))
    pl.when(odd == 1)(lambda: finish(False))


def per_device(data_cube, blanked):
    chans, rows, cols = data_cube.shape
    pix = lax.axis_size("pix")
    tiles = cols // LANES

    def move(value, axis, pairs):
        count = lax.axis_size(axis)
        return lax.ppermute(value, axis, [(a, b) for a, b in pairs if 0 <= b < count])

    def swap(value, axis, first):
        count = lax.axis_size(axis)
        pairs = [(i, i + 1 if (i - first) % 2 == 0 else i - 1) for i in range(count)]
        return move(value, axis, pairs)

    toward = [(i, i + 2 if i % 2 == 0 else i - 2) for i in range(pix)]
    back = [(i, i - 2 if i % 2 == 0 else i + 2) for i in range(pix)]
    cells, edge, edge2 = call(
        clean_cols_kernel, [f32(chans, rows, cols), f32(3, chans, cols), f32(3, chans, cols)]
    )(data_cube, blanked)
    near = swap(cells, "pix", 0)
    edge_near = move(edge, "pix", back)
    edge_far = swap(edge, "pix", 1)
    beyond = move(edge2, "pix", toward)
    near = call(
        lambda value, *rest: None,
        f32(*near.shape),
        in_specs=[ANY] * 4,
        out_specs=ANY,
        input_output_aliases={0: 0},
    )(near, edge_near, edge_far, beyond)
    far = move(near, "pix", toward)

    pair, pair_link, pair_core = call(
        pair_rows_kernel,
        [f32(chans, 32, cols), f32(HALO, 32, cols), f32(HALO, 32, cols)],
        [pltpu.VMEM((chans, 48, cols), jnp.float32)],
        micros=0.01,
    )(cells, near, edge_far, edge_near)
    pair_link = swap(pair_link, "chan", 1)
    pair_core = swap(pair_core, "chan", 0)

    outer, outer_link, outer_core = call(
        far_rows_kernel,
        [f32(chans, 16, cols), f32(HALO, 16, cols), f32(HALO, 16, cols)],
        [pltpu.VMEM((chans, 32, cols), jnp.float32)],
        micros=30.0,
    )(far, edge, beyond)
    outer_link = swap(outer_link, "chan", 1)
    outer_core = swap(outer_core, "chan", 0)

    pair_energy, core_boxes = call(
        pair_core_kernel,
        [f32(4, tiles, chans * 40, LANES), f32(4, chans // 2, rows, cols)],
        micros=2.0,
        in_specs=[VMEM, VMEM, ANY],
    )(pair, pair_core, outer)
    boxes, part, band = call(
        pair_noise_kernel,
        [
            f32(4, chans, rows, cols),
            f32(4, tiles, 2, rows, chans // 2, LANES),
            jax.ShapeDtypeStruct((2, 3 * LANES, 2 * LANES), jnp.bfloat16),
        ],
        [
            pltpu.VMEM((4, chans // 2, rows, cols), jnp.float32),
            pltpu.VMEM((4, tiles, chans * 40, LANES), jnp.float32),
        ],
        micros=3.0,
        in_specs=[VMEM] * 5 + [ANY],
    )(pair, pair_link, pair_energy, core_boxes, blanked, outer)
    far_energy = call(
        far_core_kernel,
        f32(4, tiles, chans * 24, LANES),
        in_specs=[VMEM, VMEM, ANY],
    )(outer, outer_core, part)
    return call(
        snr_kernel,
        f32(4, chans, rows, cols),
        [
            pltpu.VMEM((4, tiles, chans * 24, LANES), jnp.float32),
            pltpu.VMEM((4, tiles, chans * 24, LANES), jnp.float32),
            pltpu.VMEM((4, chans, rows, cols), jnp.float32),
            pltpu.SemaphoreType.DMA((4,)),
        ],
        micros=4.0,
        out_specs=ANY,
    )(outer, outer_link, far_energy, part, band, boxes)


def solution(mesh):
    return jax.shard_map(
        per_device,
        mesh=mesh,
        in_specs=(P("chan", "pix", None), P("pix", None)),
        out_specs=P(None, "chan", "pix", None),
        check_vma=False,
    )
```

```python
import math

import jax
import jax.numpy as jnp
from jax import lax
from jax.experimental import pallas as pl
from jax.experimental.pallas import tpu as pltpu
from jax.sharding import PartitionSpec as P

SIGMA = 3.0 / (2.0 * math.sqrt(2.0 * math.log(2.0)))
VOLUME = 14415.0
WIDTHS = (1, 3, 7, 15)
HALO = 14
LANES = 128
ANY = pl.BlockSpec(memory_space=pl.ANY)
VMEM = pl.BlockSpec(memory_space=pltpu.VMEM)


def kernel_taps():
    weights = [math.exp(-0.5 * (offset / SIGMA) ** 2) for offset in range(-3, 4)]
    total = sum(weights)
    return [weight / total for weight in weights]


def call(body, outs, scratch=(), vmem=16, micros=1.0, **specs):
    return pl.pallas_call(
        body,
        out_shape=outs,
        scratch_shapes=list(scratch),
        compiler_params=pltpu.CompilerParams(vmem_limit_bytes=vmem * 1024 * 1024),
        cost_estimate=pl.CostEstimate(
            flops=int(micros * 1e9), bytes_accessed=int(micros * 3.0e6), transcendentals=0
        ),
        **specs,
    )


def f32(*shape):
    return jax.ShapeDtypeStruct(shape, jnp.float32)


def odd_of(axis):
    return lax.axis_index(axis) % 2


def clean_cols_kernel(data, blanked, cells, edge, edge2):
    taps = kernel_taps()
    chans, rows, cols = data.shape
    even = odd_of("pix") == 0
    kept = (1 - blanked[...]).astype(jnp.float32)
    lane = lax.broadcasted_iota(jnp.int32, (rows, cols), 1)
    for c in range(chans):
        x = data[c] * kept
        acc = taps[3] * x
        for t in (1, 2, 3):
            left = jnp.where(lane >= t, pltpu.roll(x, t, 1), 0.0)
            right = jnp.where(lane < cols - t, pltpu.roll(x, cols - t, 1), 0.0)
            acc = acc + taps[3 + t] * (left + right)
        cells[c] = acc
    for r in range(3):
        top = cells[:, r, :]
        bottom = cells[:, rows - 3 + r, :]
        edge[r] = jnp.where(even, top, bottom)
        edge2[r] = jnp.where(even, bottom, top)


def smooth_rows(field, c, base, rows):
    taps = kernel_taps()
    acc = taps[3] * field[c, pl.ds(base, rows), :]
    for t in (1, 2, 3):
        acc = acc + taps[3 + t] * (
            field[c, pl.ds(base - t, rows), :] + field[c, pl.ds(base + t, rows), :]
        )
    return acc


def store_channel(c, value, full, link, core):
    chans = full.shape[0]
    skip = chans - HALO
    odd = odd_of("chan")
    full[c] = value
    if skip <= c < HALO:
        link[c - skip * odd] = value
        core[c - skip * (1 - odd)] = value
        return
    at = c if c < skip else c - skip
    first, second = (link, core) if c < skip else (core, link)

    @pl.when(odd == 0)
    def _():
        first[at] = value

    @pl.when(odd == 1)
    def _():
        second[at] = value


def pair_rows_kernel(cells, near, edge_far, edge_near, full, link, core, field):
    chans, rows, cols = cells.shape
    odd = odd_of("pix")
    even = odd == 0
    field[:, pl.ds(pl.multiple_of(8 + rows * odd, 8), rows), :] = cells[...]
    field[:, pl.ds(pl.multiple_of(8 + rows * (1 - odd), 8), rows), :] = near[...]
    for r in range(3):
        field[:, 5 + r, :] = jnp.where(even, edge_far[r], edge_near[r])
        field[:, 40 + r, :] = jnp.where(even, edge_near[r], edge_far[r])

    for c in range(chans):
        store_channel(c, smooth_rows(field, c, 8, 2 * rows), full, link, core)


def far_rows_kernel(far, edge, beyond, full1, link1, core1, full2, link2, core2, field):
    chans, rows, cols = far.shape
    at, count = lax.axis_index("pix"), lax.axis_size("pix")
    even = odd_of("pix") == 0
    present = jnp.logical_and(at > 0, at < count - 1).astype(jnp.float32)
    field[:, 8:24, :] = far[...]
    for r in range(3):
        field[:, 5 + r, :] = jnp.where(even, beyond[r], edge[r])
        field[:, 24 + r, :] = jnp.where(even, edge[r], beyond[r])

    for c in range(chans):
        value = smooth_rows(field, c, 8, rows) * present
        store_channel(c, value[:, : cols // 2], full1, link1, core1)
        store_channel(c, value[:, cols // 2 :], full2, link2, core2)


def channel_pass(own, halo, down, row, tile, energy, before, boxes, kept_at):
    chans = own.shape[0]
    stride = energy.shape[2] // chans
    at, count = lax.axis_index("chan"), lax.axis_size("chan")
    there = (at > 0 if down else at < count - 1).astype(jnp.float32)
    lanes = pl.ds(pl.multiple_of(tile * LANES, LANES), LANES)
    here = (pl.ds(pl.multiple_of(row, 8), 8), lanes)

    def s(j):
        if down and j < HALO:
            return halo[(j,) + here]
        if not down and j >= HALO + chans:
            return halo[(j - HALO - chans,) + here]
        return own[(j - HALO,) + here]

    step, first = (-1, 28) if down else (1, 15)
    one, three, seven = {}, {}, {}
    runs = [None] * 4
    for n in range(29):
        j = first + step * n
        one[j] = s(j)
        a = j - step
        if n >= 2:
            three[a] = one[a - 1] + one[a] + one[a + 1]
        b = j - 3 * step
        if n >= 6:
            seven[b] = three[b - 2] + three[b + 2] + one[b]
        if n < 14:
            continue
        j -= 7 * step
        fifteen = seven[j - 4] + seven[j + 4] + one[j]
        k = j - 7
        c = k if down else k - 14
        for w, box in enumerate((one[j], three[j], seven[j], fifteen)):
            if kept_at is not None and 7 <= k < 23:
                at_rows = pl.ds(pl.multiple_of(kept_at, 8), 8)
                boxes[w, k - 7 if down else k - 15, at_rows, lanes] = box
            square = box * box
            if k < 7 or k >= 23:
                square = square * there
            runs[w] = square if runs[w] is None else runs[w] + square
            at_c = (w, tile, pl.ds(pl.multiple_of(c * stride + row, 8), 8), slice(None))
            if before is not None and 1 <= c <= 14:
                energy[at_c] = before[at_c] + runs[w]
            else:
                energy[at_c] = runs[w]
    if before is not None:
        c = 15 if down else 0
        for w in range(4):
            at_c = (w, tile, pl.ds(pl.multiple_of(c * stride + row, 8), 8), slice(None))
            energy[at_c] = before[at_c]


def strips(own, halo, core_side, energy, before, boxes):
    chans, tall, cols = own.shape
    odd = odd_of("chan")
    tiles = cols // LANES
    own_row = 16 * odd_of("pix")

    def run(down):
        def both(n, carry):
            tile, i = n // 2, n % 2
            if tall == 32:
                channel_pass(own, halo, down, own_row + 8 * i, tile, energy, before, boxes, 8 * i)
                channel_pass(own, halo, down, 16 - own_row + 8 * i, tile, energy, before, None, None)
            else:
                channel_pass(own, halo, down, 8 * i, tile, energy, before, None, None)
            return carry

        lax.fori_loop(0, 2 * tiles, both, 0)

    pl.when(odd == 0)(lambda: run(not core_side))
    pl.when(odd == 1)(lambda: run(core_side))


def pair_core_kernel(own, core, after, energy, boxes):
    strips(own, core, True, energy, None, boxes)


def far_core_kernel(own, core, after, energy):
    strips(own, core, True, energy, None, None)


def two_terms(sums, w):
    tiles, height = sums.shape[1:3]
    firsts, seconds = [], []
    for tile in range(tiles):
        value = sums[w, tile].reshape(16, height // 16, LANES)[:, :16].reshape(256, LANES)
        firsts.append(value.astype(jnp.bfloat16))
        seconds.append((value - firsts[-1].astype(jnp.float32)).astype(jnp.bfloat16))
    return firsts, seconds


def for_parity(odd, body):
    def loop(even):
        def step(w, carry):
            body(w, even)
            return carry

        lax.fori_loop(0, 4, step, 0)

    pl.when(odd == 0)(lambda: loop(True))
    pl.when(odd == 1)(lambda: loop(False))


def pair_noise_kernel(
    own, link, before, core_boxes, blanked, after, boxes, sums, band, link_boxes, energy
):
    chans, tall, cols = own.shape
    rows = tall // 2
    odd = odd_of("pix")
    strips(own, link, False, energy, before, link_boxes)
    low = pl.ds(8 * odd_of("chan"), 8)
    high = pl.ds(8 - 8 * odd_of("chan"), 8)
    kept = (1 - blanked[...]).astype(jnp.float32)
    for w, width in enumerate(WIDTHS):
        factor = (kept * (1.0 / width))[None]
        boxes[w, low] = link_boxes[w] * factor
        boxes[w, high] = core_boxes[w] * factor

    stride = energy.shape[2] // chans

    def row_windows(w, even):
        for half in range(2):
            for tile in range(cols // LANES):

                def e(i):
                    return energy[w, tile, pl.ds(half * 8 * stride + i, 8, stride=stride), :]

                first = 0 if even else rows
                run = e(first)
                for i in range(1, rows):
                    run = run + e(first + i)
                for d in range(rows):
                    if d > 0:
                        run = run + e(15 + d if even else 16 - d)
                    sums[w, tile, half, d if even else 15 - d] = run

    for_parity(odd, row_windows)
    for h in range(2):
        i = lax.broadcasted_iota(jnp.int32, band.shape[1:], 0) + h * LANES
        j = lax.broadcasted_iota(jnp.int32, band.shape[1:], 1) + h * 2 * LANES
        band[h] = (jnp.abs(i - j) <= 15).astype(jnp.float32).astype(jnp.bfloat16)


def far_windows(w, even, first, part, sums, energy):
    stride = energy.shape[2] // 16
    for half in range(2):
        for tile in range(sums.shape[1]):
            run = None
            for d in range(16):
                if d > 0:
                    i = 16 - d if even else d - 1
                    e = energy[w, tile, pl.ds(half * 8 * stride + i, 8, stride=stride), :]
                    run = e if run is None else run + e
                row = 15 - d if even else d
                value = part[w, first + tile, half, row]
                at = pl.ds(half * 8 * stride + row, 8, stride=stride)
                sums[w, tile, at, :] = value if run is None else value + run


def far_first_kernel(own, link, before, part, sums, energy):
    strips(own, link, False, energy, before, None)
    for_parity(odd_of("pix"), lambda w, even: far_windows(w, even, 0, part, sums, energy))


def snr_kernel(
    own, link, before, part, first, band, boxes, out, energy, sums, ready, sems
):
    chans, rows = boxes.shape[1:3]
    odd = odd_of("pix")
    strips(own, link, False, energy, before, None)

    def finish(even):
        copies = []
        for w, width in enumerate(WIDTHS):
            far_windows(w, even, 2, part, sums, energy)
            firsts, seconds = two_terms(first, w)
            more = two_terms(sums, w)
            firsts, seconds = firsts + more[0], seconds + more[1]
            for h in range(2):
                both = jnp.concatenate(firsts[h : h + 3] + seconds[h : h + 3], axis=1)
                ones = jnp.concatenate([band[h], band[h]], axis=0)
                total = jnp.dot(both, ones, preferred_element_type=jnp.float32)
                scale = lax.rsqrt(total * (1.0 / (VOLUME * width * width)) + 1e-5)
                lanes = slice(h * 2 * LANES, (h + 1) * 2 * LANES)
                ready[w, :, :, lanes] = boxes[w, :, :, lanes] * scale.reshape(chans, rows, -1)
            copies.append(pltpu.make_async_copy(ready.at[w], out.at[w], sems.at[w]))
            copies[-1].start()
        for copy in copies:
            copy.wait()

    pl.when(odd == 0)(lambda: finish(True))
    pl.when(odd == 1)(lambda: finish(False))


def per_device(data_cube, blanked):
    chans, rows, cols = data_cube.shape
    pix = lax.axis_size("pix")
    tiles = cols // LANES

    def move(value, axis, pairs):
        count = lax.axis_size(axis)
        return lax.ppermute(value, axis, [(a, b) for a, b in pairs if 0 <= b < count])

    def swap(value, axis, first):
        count = lax.axis_size(axis)
        pairs = [(i, i + 1 if (i - first) % 2 == 0 else i - 1) for i in range(count)]
        return move(value, axis, pairs)

    toward = [(i, i + 2 if i % 2 == 0 else i - 2) for i in range(pix)]
    back = [(i, i - 2 if i % 2 == 0 else i + 2) for i in range(pix)]
    cells, edge, edge2 = call(
        clean_cols_kernel, [f32(chans, rows, cols), f32(3, chans, cols), f32(3, chans, cols)]
    )(data_cube, blanked)
    near = swap(cells, "pix", 0)
    edge_near = move(edge, "pix", back)
    edge_far = swap(edge, "pix", 1)
    beyond = move(edge2, "pix", toward)
    near = call(
        lambda value, *rest: None,
        f32(*near.shape),
        in_specs=[ANY] * 4,
        out_specs=ANY,
        input_output_aliases={0: 0},
    )(near, edge_near, edge_far, beyond)
    far = move(near, "pix", toward)

    pair, pair_link, pair_core = call(
        pair_rows_kernel,
        [f32(chans, 32, cols), f32(HALO, 32, cols), f32(HALO, 32, cols)],
        [pltpu.VMEM((chans, 48, cols), jnp.float32)],
        micros=0.01,
    )(cells, near, edge_far, edge_near)
    pair_link = swap(pair_link, "chan", 1)
    pair_core = swap(pair_core, "chan", 0)

    half = cols // 2
    outer, link1, core1, outer2, link2, core2 = call(
        far_rows_kernel,
        [f32(chans, 16, half), f32(HALO, 16, half), f32(HALO, 16, half)] * 2,
        [pltpu.VMEM((chans, 32, cols), jnp.float32)],
        micros=30.0,
    )(far, edge, beyond)
    link1, core1 = swap(link1, "chan", 1), swap(core1, "chan", 0)
    link2, core2 = swap(link2, "chan", 1), swap(core2, "chan", 0)

    pair_energy, core_boxes = call(
        pair_core_kernel,
        [f32(4, tiles, chans * 40, LANES), f32(4, chans // 2, rows, cols)],
        micros=2.0,
        in_specs=[VMEM, VMEM, ANY],
    )(pair, pair_core, outer)
    boxes, part, band = call(
        pair_noise_kernel,
        [
            f32(4, chans, rows, cols),
            f32(4, tiles, 2, rows, chans // 2, LANES),
            jax.ShapeDtypeStruct((2, 3 * LANES, 2 * LANES), jnp.bfloat16),
        ],
        [
            pltpu.VMEM((4, chans // 2, rows, cols), jnp.float32),
            pltpu.VMEM((4, tiles, chans * 40, LANES), jnp.float32),
        ],
        micros=3.0,
        in_specs=[VMEM] * 5 + [ANY],
    )(pair, pair_link, pair_energy, core_boxes, blanked, outer)
    sums = f32(4, tiles // 2, chans * 24, LANES)
    scratch = pltpu.VMEM(sums.shape, jnp.float32)
    ordered = dict(in_specs=[VMEM, VMEM, ANY])
    energy1 = call(far_core_kernel, sums, **ordered)(outer, core1, part)
    energy2 = call(far_core_kernel, sums, **ordered)(outer2, core2, part)
    first = call(far_first_kernel, sums, [scratch])(outer, link1, energy1, part)
    return call(
        snr_kernel,
        f32(4, chans, rows, cols),
        [
            scratch,
            scratch,
            pltpu.VMEM((4, chans, rows, cols), jnp.float32),
            pltpu.SemaphoreType.DMA((4,)),
        ],
        micros=4.0,
        out_specs=ANY,
    )(outer2, link2, energy2, part, first, band, boxes)


def solution(mesh):
    return jax.shard_map(
        per_device,
        mesh=mesh,
        in_specs=(P("chan", "pix", None), P("pix", None)),
        out_specs=P(None, "chan", "pix", None),
        check_vma=False,
    )
```

```python
import math

import jax
import jax.numpy as jnp
from jax import lax
from jax.experimental import pallas as pl
from jax.experimental.pallas import tpu as pltpu
from jax.sharding import PartitionSpec as P

SIGMA = 3.0 / (2.0 * math.sqrt(2.0 * math.log(2.0)))
VOLUME = 14415.0
WIDTHS = (1, 3, 7, 15)
HALO = 14
LANES = 128
ANY = pl.BlockSpec(memory_space=pl.ANY)
VMEM = pl.BlockSpec(memory_space=pltpu.VMEM)


def kernel_taps():
    weights = [math.exp(-0.5 * (offset / SIGMA) ** 2) for offset in range(-3, 4)]
    total = sum(weights)
    return [weight / total for weight in weights]


def call(body, outs, scratch=(), vmem=16, micros=1.0, **specs):
    return pl.pallas_call(
        body,
        out_shape=outs,
        scratch_shapes=list(scratch),
        compiler_params=pltpu.CompilerParams(vmem_limit_bytes=vmem * 1024 * 1024),
        cost_estimate=pl.CostEstimate(
            flops=int(micros * 1e9), bytes_accessed=int(micros * 3.0e6), transcendentals=0
        ),
        **specs,
    )


def f32(*shape):
    return jax.ShapeDtypeStruct(shape, jnp.float32)


def odd_of(axis):
    return lax.axis_index(axis) % 2


def clean_cols_kernel(data, blanked, cells, second, edge, edge2):
    taps = kernel_taps()
    chans, rows, cols = data.shape
    even = odd_of("pix") == 0
    kept = (1 - blanked[...]).astype(jnp.float32)
    lane = lax.broadcasted_iota(jnp.int32, (rows, cols), 1)
    for c in range(chans):
        x = data[c] * kept
        acc = taps[3] * x
        for t in (1, 2, 3):
            left = jnp.where(lane >= t, pltpu.roll(x, t, 1), 0.0)
            right = jnp.where(lane < cols - t, pltpu.roll(x, cols - t, 1), 0.0)
            acc = acc + taps[3 + t] * (left + right)
        cells[c] = acc
        second[c] = acc[:, cols - second.shape[2] :]
    for r in range(3):
        top = cells[:, r, :]
        bottom = cells[:, rows - 3 + r, :]
        edge[r] = jnp.where(even, top, bottom)
        edge2[r] = jnp.where(even, bottom, top)


def smooth_rows(field, c, base, rows):
    taps = kernel_taps()
    acc = taps[3] * field[c, pl.ds(base, rows), :]
    for t in (1, 2, 3):
        acc = acc + taps[3 + t] * (
            field[c, pl.ds(base - t, rows), :] + field[c, pl.ds(base + t, rows), :]
        )
    return acc


def store_channel(c, value, full, link, core):
    chans = full.shape[0]
    skip = chans - HALO
    odd = odd_of("chan")
    full[c] = value
    if skip <= c < HALO:
        link[c - skip * odd] = value
        core[c - skip * (1 - odd)] = value
        return
    at = c if c < skip else c - skip
    first, second = (link, core) if c < skip else (core, link)

    @pl.when(odd == 0)
    def _():
        first[at] = value

    @pl.when(odd == 1)
    def _():
        second[at] = value


def pair_rows_kernel(cells, near, edge_far, edge_near, full, link, core, field):
    chans, rows, cols = cells.shape
    odd = odd_of("pix")
    even = odd == 0
    field[:, pl.ds(pl.multiple_of(8 + rows * odd, 8), rows), :] = cells[...]
    field[:, pl.ds(pl.multiple_of(8 + rows * (1 - odd), 8), rows), :] = near[...]
    for r in range(3):
        field[:, 5 + r, :] = jnp.where(even, edge_far[r], edge_near[r])
        field[:, 40 + r, :] = jnp.where(even, edge_near[r], edge_far[r])

    for c in range(chans):
        store_channel(c, smooth_rows(field, c, 8, 2 * rows), full, link, core)


def far_rows_kernel(
    far1, far2, edge, beyond, full1, link1, core1, full2, link2, core2, field
):
    chans, rows, half = far1.shape
    at, count = lax.axis_index("pix"), lax.axis_size("pix")
    even = odd_of("pix") == 0
    present = jnp.logical_and(at > 0, at < count - 1).astype(jnp.float32)
    field[:, 8:24, :half] = far1[...]
    field[:, 8:24, half:] = far2[...]
    for r in range(3):
        field[:, 5 + r, :] = jnp.where(even, beyond[r], edge[r])
        field[:, 24 + r, :] = jnp.where(even, edge[r], beyond[r])

    for c in range(chans):
        value = smooth_rows(field, c, 8, rows) * present
        store_channel(c, value[:, :half], full1, link1, core1)
        store_channel(c, value[:, half:], full2, link2, core2)


def channel_pass(own, halo, down, row, tile, energy, before, boxes, kept_at):
    chans = own.shape[0]
    stride = energy.shape[2] // chans
    at, count = lax.axis_index("chan"), lax.axis_size("chan")
    there = (at > 0 if down else at < count - 1).astype(jnp.float32)
    lanes = pl.ds(pl.multiple_of(tile * LANES, LANES), LANES)
    here = (pl.ds(pl.multiple_of(row, 8), 8), lanes)

    def s(j):
        if down and j < HALO:
            return halo[(j,) + here]
        if not down and j >= HALO + chans:
            return halo[(j - HALO - chans,) + here]
        return own[(j - HALO,) + here]

    step, first = (-1, 28) if down else (1, 15)
    one, three, seven = {}, {}, {}
    runs = [None] * 4
    for n in range(29):
        j = first + step * n
        one[j] = s(j)
        a = j - step
        if n >= 2:
            three[a] = one[a - 1] + one[a] + one[a + 1]
        b = j - 3 * step
        if n >= 6:
            seven[b] = three[b - 2] + three[b + 2] + one[b]
        if n < 14:
            continue
        j -= 7 * step
        fifteen = seven[j - 4] + seven[j + 4] + one[j]
        k = j - 7
        c = k if down else k - 14
        for w, box in enumerate((one[j], three[j], seven[j], fifteen)):
            if kept_at is not None and 7 <= k < 23:
                at_rows = pl.ds(pl.multiple_of(kept_at, 8), 8)
                boxes[w, k - 7 if down else k - 15, at_rows, lanes] = box
            square = box * box
            if k < 7 or k >= 23:
                square = square * there
            runs[w] = square if runs[w] is None else runs[w] + square
            at_c = (w, tile, pl.ds(pl.multiple_of(c * stride + row, 8), 8), slice(None))
            if before is not None and 1 <= c <= 14:
                energy[at_c] = before[at_c] + runs[w]
            else:
                energy[at_c] = runs[w]
    if before is not None:
        c = 15 if down else 0
        for w in range(4):
            at_c = (w, tile, pl.ds(pl.multiple_of(c * stride + row, 8), 8), slice(None))
            energy[at_c] = before[at_c]


def strips(own, halo, core_side, energy, before, boxes):
    chans, tall, cols = own.shape
    odd = odd_of("chan")
    tiles = cols // LANES
    own_row = 16 * odd_of("pix")

    def run(down):
        def both(n, carry):
            tile, i = n // 2, n % 2
            if tall == 32:
                channel_pass(own, halo, down, own_row + 8 * i, tile, energy, before, boxes, 8 * i)
                channel_pass(own, halo, down, 16 - own_row + 8 * i, tile, energy, before, None, None)
            else:
                channel_pass(own, halo, down, 8 * i, tile, energy, before, None, None)
            return carry

        lax.fori_loop(0, 2 * tiles, both, 0)

    pl.when(odd == 0)(lambda: run(not core_side))
    pl.when(odd == 1)(lambda: run(core_side))


def pair_core_kernel(own, core, after, energy, boxes):
    strips(own, core, True, energy, None, boxes)


def far_core_kernel(own, core, after, energy):
    strips(own, core, True, energy, None, None)


def two_terms(sums, w):
    tiles, height = sums.shape[1:3]
    firsts, seconds = [], []
    for tile in range(tiles):
        value = sums[w, tile].reshape(16, height // 16, LANES)[:, :16].reshape(256, LANES)
        firsts.append(value.astype(jnp.bfloat16))
        seconds.append((value - firsts[-1].astype(jnp.float32)).astype(jnp.bfloat16))
    return firsts, seconds


def for_parity(odd, body):
    def loop(even):
        def step(w, carry):
            body(w, even)
            return carry

        lax.fori_loop(0, 4, step, 0)

    pl.when(odd == 0)(lambda: loop(True))
    pl.when(odd == 1)(lambda: loop(False))


def pair_noise_kernel(
    own, link, before, core_boxes, blanked, after, boxes, sums, band, link_boxes, energy
):
    chans, tall, cols = own.shape
    rows = tall // 2
    odd = odd_of("pix")
    strips(own, link, False, energy, before, link_boxes)
    low = pl.ds(8 * odd_of("chan"), 8)
    high = pl.ds(8 - 8 * odd_of("chan"), 8)
    kept = (1 - blanked[...]).astype(jnp.float32)
    for w, width in enumerate(WIDTHS):
        factor = (kept * (1.0 / width))[None]
        boxes[w, low] = link_boxes[w] * factor
        boxes[w, high] = core_boxes[w] * factor

    stride = energy.shape[2] // chans

    def row_windows(w, even):
        for half in range(2):
            for tile in range(cols // LANES):

                def e(i):
                    return energy[w, tile, pl.ds(half * 8 * stride + i, 8, stride=stride), :]

                first = 0 if even else rows
                run = e(first)
                for i in range(1, rows):
                    run = run + e(first + i)
                for d in range(rows):
                    if d > 0:
                        run = run + e(15 + d if even else 16 - d)
                    sums[w, tile, half, d if even else 15 - d] = run

    for_parity(odd, row_windows)
    for h in range(2):
        i = lax.broadcasted_iota(jnp.int32, band.shape[1:], 0) + h * LANES
        j = lax.broadcasted_iota(jnp.int32, band.shape[1:], 1) + h * 2 * LANES
        band[h] = (jnp.abs(i - j) <= 15).astype(jnp.float32).astype(jnp.bfloat16)


def far_windows(w, even, first, part, sums, energy):
    stride = energy.shape[2] // 16
    for half in range(2):
        for tile in range(sums.shape[1]):
            run = None
            for d in range(16):
                if d > 0:
                    i = 16 - d if even else d - 1
                    e = energy[w, tile, pl.ds(half * 8 * stride + i, 8, stride=stride), :]
                    run = e if run is None else run + e
                row = 15 - d if even else d
                value = part[w, first + tile, half, row]
                at = pl.ds(half * 8 * stride + row, 8, stride=stride)
                sums[w, tile, at, :] = value if run is None else value + run


def far_first_kernel(own, link, before, part, sums, energy):
    strips(own, link, False, energy, before, None)
    for_parity(odd_of("pix"), lambda w, even: far_windows(w, even, 0, part, sums, energy))


def snr_kernel(
    own, link, before, part, first, band, boxes, out, energy, sums, ready, sems
):
    chans, rows = boxes.shape[1:3]
    odd = odd_of("pix")
    strips(own, link, False, energy, before, None)

    def finish(even):
        copies = []
        for w, width in enumerate(WIDTHS):
            far_windows(w, even, 2, part, sums, energy)
            firsts, seconds = two_terms(first, w)
            more = two_terms(sums, w)
            firsts, seconds = firsts + more[0], seconds + more[1]
            for h in range(2):
                both = jnp.concatenate(firsts[h : h + 3] + seconds[h : h + 3], axis=1)
                ones = jnp.concatenate([band[h], band[h]], axis=0)
                total = jnp.dot(both, ones, preferred_element_type=jnp.float32)
                scale = lax.rsqrt(total * (1.0 / (VOLUME * width * width)) + 1e-5)
                lanes = slice(h * 2 * LANES, (h + 1) * 2 * LANES)
                ready[w, :, :, lanes] = boxes[w, :, :, lanes] * scale.reshape(chans, rows, -1)
            copies.append(pltpu.make_async_copy(ready.at[w], out.at[w], sems.at[w]))
            copies[-1].start()
        for copy in copies:
            copy.wait()

    pl.when(odd == 0)(lambda: finish(True))
    pl.when(odd == 1)(lambda: finish(False))


def per_device(data_cube, blanked):
    chans, rows, cols = data_cube.shape
    pix = lax.axis_size("pix")
    tiles = cols // LANES

    def move(value, axis, pairs):
        count = lax.axis_size(axis)
        return lax.ppermute(value, axis, [(a, b) for a, b in pairs if 0 <= b < count])

    def swap(value, axis, first):
        count = lax.axis_size(axis)
        pairs = [(i, i + 1 if (i - first) % 2 == 0 else i - 1) for i in range(count)]
        return move(value, axis, pairs)

    toward = [(i, i + 2 if i % 2 == 0 else i - 2) for i in range(pix)]
    back = [(i, i - 2 if i % 2 == 0 else i + 2) for i in range(pix)]
    half = cols // 2
    cells, right, edge, edge2 = call(
        clean_cols_kernel,
        [f32(chans, rows, cols), f32(chans, rows, half), f32(3, chans, cols), f32(3, chans, cols)],
    )(data_cube, blanked)
    near = swap(cells, "pix", 0)
    far_right = swap(move(right, "pix", back), "pix", 0)
    edge_near = move(edge, "pix", back)
    edge_far = swap(edge, "pix", 1)
    beyond = move(edge2, "pix", toward)

    def left_half(value, *rest):
        rest[-1][...] = value[:, :, : rest[-1].shape[2]]

    near_left = call(left_half, f32(chans, rows, half), in_specs=[VMEM] + [ANY] * 3)(
        near, edge_near, edge_far, beyond
    )
    far_left = move(near_left, "pix", toward)

    pair, pair_link, pair_core = call(
        pair_rows_kernel,
        [f32(chans, 32, cols), f32(HALO, 32, cols), f32(HALO, 32, cols)],
        [pltpu.VMEM((chans, 48, cols), jnp.float32)],
        micros=0.01,
    )(cells, near, edge_far, edge_near)
    pair_link = swap(pair_link, "chan", 1)
    pair_core = swap(pair_core, "chan", 0)

    outer, link1, core1, outer2, link2, core2 = call(
        far_rows_kernel,
        [f32(chans, 16, half), f32(HALO, 16, half), f32(HALO, 16, half)] * 2,
        [pltpu.VMEM((chans, 32, cols), jnp.float32)],
        micros=30.0,
    )(far_left, far_right, edge, beyond)
    link1, core1 = swap(link1, "chan", 1), swap(core1, "chan", 0)
    link2, core2 = swap(link2, "chan", 1), swap(core2, "chan", 0)

    pair_energy, core_boxes = call(
        pair_core_kernel,
        [f32(4, tiles, chans * 40, LANES), f32(4, chans // 2, rows, cols)],
        micros=2.0,
        in_specs=[VMEM, VMEM, ANY],
    )(pair, pair_core, outer)
    boxes, part, band = call(
        pair_noise_kernel,
        [
            f32(4, chans, rows, cols),
            f32(4, tiles, 2, rows, chans // 2, LANES),
            jax.ShapeDtypeStruct((2, 3 * LANES, 2 * LANES), jnp.bfloat16),
        ],
        [
            pltpu.VMEM((4, chans // 2, rows, cols), jnp.float32),
            pltpu.VMEM((4, tiles, chans * 40, LANES), jnp.float32),
        ],
        micros=3.0,
        in_specs=[VMEM] * 5 + [ANY],
    )(pair, pair_link, pair_energy, core_boxes, blanked, outer)
    sums = f32(4, tiles // 2, chans * 24, LANES)
    scratch = pltpu.VMEM(sums.shape, jnp.float32)
    ordered = dict(in_specs=[VMEM, VMEM, ANY])
    energy1 = call(far_core_kernel, sums, **ordered)(outer, core1, part)
    energy2 = call(far_core_kernel, sums, **ordered)(outer2, core2, part)
    first = call(far_first_kernel, sums, [scratch])(outer, link1, energy1, part)
    return call(
        snr_kernel,
        f32(4, chans, rows, cols),
        [
            scratch,
            scratch,
            pltpu.VMEM((4, chans, rows, cols), jnp.float32),
            pltpu.SemaphoreType.DMA((4,)),
        ],
        micros=4.0,
        out_specs=ANY,
    )(outer2, link2, energy2, part, first, band, boxes)


def solution(mesh):
    return jax.shard_map(
        per_device,
        mesh=mesh,
        in_specs=(P("chan", "pix", None), P("pix", None)),
        out_specs=P(None, "chan", "pix", None),
        check_vma=False,
    )
```
